128 devices in a mesh: grp: 8 (over y, core), dev: 16 (over x, z).
Axes of the slice: x: 4, y: 4, z: 4, core: 2. Of those that a mesh axis runs over, the one named last changes fastest.
Arguments:
- modes: bfloat16 [32, 2097152], P(None, ('grp', 'dev')), may hold values from -6 to 6
- geometry: float32 [4, 2097152], P(None, ('grp', 'dev')), may hold values from -2.4 to 2.4, as said below
- pair_list: int32 [16384, 2], P(('grp', 'dev')), may hold values from 0 to 8191, as said below
- pair_kind: int32 [16384], P(('grp', 'dev')), may hold values from 0 to 2, as said below
Outputs:
- added: float32 [32, 2097152], P(None, ('grp', 'dev'))
The draws below stay inside these ranges and needn't reach their ends.
Inputs may be any that keep to these rules, and one draw needn't show every extreme that they name: `pair_list`: cluster ids. Of the 256 cluster ids in the slots of one device (empty slots included), at most 2 lie on any one device (cluster c lies on device c // 64 of grp+dev), and every device that holds one of them holds exactly 2. `pair_kind`: on each device the live slots come first; some device has all 128 slots live. `geometry`: rows 0 to 2 lie in -2.4 to 2.4; row 3 lies in 0.1 to 2.
All inputs are finite; a program needn't handle non-finite values.
Results may differ from the reference program's by a relative error of at most 0.0029.
Values may be sent and summed in bfloat16 or wider, within the bound.
A program may use at most 64 MiB of HBM per device.

```python
import math
import jax
import jax.numpy as jnp
from jax import lax

M = 32
P_SIZE = 256
C_DEV = 64
SLOTS_DEV = 128
CAP = 2
CLUSTERS = 8192
PANELS = 2097152
PAIRS = 16384
N_GRP = 8
N_DEV = 16


def draw_geometry(key, part):
    key = jax.random.fold_in(key, 5)
    first_key, second_key = jax.random.split(key)
    coords = jnp.clip(0.6 * jax.random.normal(first_key, (3, PANELS), jnp.float32), -2.4, 2.4)
    areas = jnp.exp(jax.random.uniform(second_key, (1, PANELS), jnp.float32, math.log(0.1), math.log(2.0)))
    areas = jnp.clip(areas, 0.1, 2.0)
    return jnp.concatenate([coords, areas], axis=0).astype(jnp.float32)


def draw_pair_list(key, part):
    key = jax.random.fold_in(key, 11)
    devices = N_GRP * N_DEV
    end_count = 2 * SLOTS_DEV
    run_count = (end_count + CAP - 1) // CAP

    def one_device(device_key):
        first_key, second_key, third_key = jax.random.split(device_key, 3)
        holders = jax.random.permutation(first_key, devices)[:run_count]
        per_end = jnp.repeat(holders, CAP)[:end_count]
        shuffle = jax.random.permutation(second_key, end_count)
        per_end = per_end[shuffle]
        local_id = jax.random.randint(third_key, (end_count,), 0, C_DEV)
        return (per_end * C_DEV + local_id).reshape(SLOTS_DEV, 2)
    device_keys = jax.random.split(key, devices)
    pair_ids = jax.vmap(one_device)(device_keys)
    return pair_ids.reshape(SLOTS_DEV * devices, 2).astype(jnp.int32)


def draw_pair_kind(key, part):
    key = jax.random.fold_in(key, 12)
    devices = N_GRP * N_DEV
    first_key, second_key, third_key = jax.random.split(key, 3)
    counts = jax.random.randint(first_key, (devices,), SLOTS_DEV // 4, SLOTS_DEV // 2 + 1)
    busiest = jax.random.randint(second_key, (), 0, devices)
    counts = jnp.where(jnp.arange(devices) == busiest, SLOTS_DEV, counts)
    kinds = jax.random.randint(third_key, (devices, SLOTS_DEV), 1, 3)
    live_mask = jnp.arange(SLOTS_DEV)[None, :] < counts[:, None]
    return jnp.where(live_mask, kinds, 0).reshape(devices * SLOTS_DEV).astype(jnp.int32)


def levels(stream_key, dims, pieces, low, largest):
    loudness = 1.0
    for axis_at, blocks in pieces:
        draws = jax.random.uniform(jax.random.fold_in(jax.random.fold_in(stream_key, 6), axis_at), (blocks,), jnp.float32, low / len(pieces), largest / len(pieces))
        loudness = loudness * jnp.repeat(jnp.exp(draws), dims[axis_at] // blocks).reshape((-1,) + (1,) * (len(dims) - 1 - axis_at))
    return loudness


def scatter_about(own_key, dims, width, limit, shards=(), dtype=jnp.bfloat16):
    loudness = levels(own_key, dims, shards, -0.22, 0.18) if shards else 1.0
    entries = jax.random.normal(own_key, dims, jnp.float32) * width * loudness
    return jnp.minimum(jnp.maximum(entries, -limit), limit).astype(dtype)


def setup_inputs(seed: int = 0) -> dict:
    key_list = jax.random.split(jax.random.key(seed), 5)
    return {
        "modes": scatter_about(key_list[0], (M, PANELS), 1.0, 6.0, ((1, 128),)),
        "geometry": draw_geometry(jax.random.fold_in(key_list[4], 71), 0),
        "pair_list": draw_pair_list(jax.random.fold_in(key_list[4], 71), 0),
        "pair_kind": draw_pair_kind(jax.random.fold_in(key_list[4], 71), 0),
    }


KERNEL_SCALE = 0.25 / math.pi

def pair_kernel(left_geo, right_geo, factor):
    distance = (left_geo[:, 0, :, None] - right_geo[:, 0, None, :]) ** 2
    distance = distance + (left_geo[:, 1, :, None] - right_geo[:, 1, None, :]) ** 2
    distance = distance + (left_geo[:, 2, :, None] - right_geo[:, 2, None, :]) ** 2
    smooth = factor[:, None, None] * (left_geo[:, 3, :, None] + right_geo[:, 3, None, :])
    return (KERNEL_SCALE / jnp.sqrt(distance + smooth)).astype(jnp.bfloat16)

def reference(modes, geometry, pair_list, pair_kind):
    mode_blocks = modes.reshape(M, CLUSTERS, P_SIZE).transpose(1, 0, 2)
    geo_blocks = geometry.reshape(4, CLUSTERS, P_SIZE).transpose(1, 0, 2)
    block_ids = pair_list.reshape(PAIRS // 8, 8, 2)
    block_kinds = pair_kind.reshape(PAIRS // 8, 8)

    def step(block_index, total):
        pair_ids = block_ids[block_index]
        kinds = block_kinds[block_index]
        left_ids = pair_ids[:, 0].astype(jnp.int32)
        right_ids = pair_ids[:, 1].astype(jnp.int32)

        def work(carried):
            factor = jnp.where(kinds == 2, 0.1, 1.0).astype(jnp.float32)
            keep_left = (kinds > 0).astype(jnp.float32)
            keep_right = keep_left * (left_ids != right_ids).astype(jnp.float32)
            kernel = pair_kernel(geo_blocks[left_ids], geo_blocks[right_ids], factor).astype(jnp.float32)
            left_modes = mode_blocks[left_ids].astype(jnp.float32)
            right_modes = mode_blocks[right_ids].astype(jnp.float32)
            into_left = jnp.einsum('bmq,bpq->bmp', right_modes, kernel, precision=lax.Precision.HIGHEST)
            into_right = jnp.einsum('bmp,bpq->bmq', left_modes, kernel, precision=lax.Precision.HIGHEST)
            carried = carried.at[left_ids].add(into_left * keep_left[:, None, None])
            return carried.at[right_ids].add(into_right * keep_right[:, None, None])
        return lax.cond(jnp.any(kinds > 0), work, lambda carried: carried, total)
    total = lax.fori_loop(0, PAIRS // 8, step, jnp.zeros((CLUSTERS, M, P_SIZE), jnp.float32))
    return total.transpose(1, 0, 2).reshape(M, PANELS)
```

```python
import functools
import math

import jax
import jax.numpy as jnp
from jax import lax
from jax.experimental import pallas as pl
from jax.experimental.pallas import tpu as pltpu
from jax.sharding import PartitionSpec as P

P_SIZE = 256
MODES = 32
KEY = 16
FOUR_PI = 4.0 * math.pi
MESH = pl.DeviceIdType.MESH


def split_two(value):
    high = value.astype(jnp.bfloat16)
    low = (value - high.astype(jnp.float32)).astype(jnp.bfloat16)
    return high, low


def split_three(value):
    high = value.astype(jnp.bfloat16)
    rest = value - high.astype(jnp.float32)
    mid = rest.astype(jnp.bfloat16)
    low = (rest - mid.astype(jnp.float32)).astype(jnp.bfloat16)
    return high, mid, low


def exchange_kernel(
    groups, members, side,
    code_ref, request_ref, modes_ref, geo_ref,
    back_ref, asked_ref,
    asked_smem, mode_blocks, geo_blocks, geo_stage, geo_got, mode_stage, mode_got, mode_back,
    left_xyz, right_xyz, left_norm, right_norm,
    send_sems, recv_sems, local_sem,
):
    devices = groups * members
    others = devices - 1
    grp = lax.axis_index("grp")
    dev = lax.axis_index("dev")
    me = grp * members + dev
    halves = groups // 2

    def partner_of(step):
        shift = (step * 45) % devices
        dg, dv = shift // members, shift % members
        y = (grp // 2 + dg // 2) % halves
        core = (grp + dg) % 2
        x = (dev // side + dv // side) % side
        z = (dev + dv) % side
        return y * 2 + core, x * side + z

    barrier = pltpu.get_barrier_semaphore()

    @pl.loop(1, devices)
    def _(step):
        pl.semaphore_signal(barrier, inc=1, device_id=partner_of(step), device_id_type=MESH)

    for cluster in range(mode_blocks.shape[0]):
        mode_blocks[cluster] = modes_ref[:, cluster * P_SIZE : (cluster + 1) * P_SIZE]
        geo_blocks[cluster] = geo_ref[:, cluster * P_SIZE : (cluster + 1) * P_SIZE]

    pl.semaphore_wait(barrier, others)

    def send(source, target, which, place):
        pltpu.make_async_remote_copy(
            src_ref=source, dst_ref=target,
            send_sem=send_sems.at[which], recv_sem=recv_sems.at[which],
            device_id=place, device_id_type=MESH,
        ).start()

    def drain(source, target, which):
        return pltpu.make_async_remote_copy(
            src_ref=source, dst_ref=target,
            send_sem=send_sems.at[which], recv_sem=recv_sems.at[which],
            device_id=(grp, dev), device_id_type=MESH,
        )

    @pl.loop(1, devices)
    def _(step):
        to_grp, to_dev = partner_of(step)
        to = to_grp * members + to_dev
        send(request_ref.at[to], asked_ref.at[me], 0, (to_grp, to_dev))

    asked_ref[me] = request_ref[me]
    requests = drain(request_ref.at[pl.ds(0, others)], asked_ref.at[pl.ds(0, others)], 0)
    requests.wait_recv()
    local = pltpu.make_async_copy(asked_ref, asked_smem, local_sem)
    local.start()
    local.wait()

    def wanted(to, rank):
        return asked_smem[to, 0, rank] & 63

    @pl.loop(1, devices)
    def _(step):
        to_grp, to_dev = partner_of(step)
        to = to_grp * members + to_dev
        geo_stage[to, 0:4] = geo_blocks[wanted(to, 0)]
        geo_stage[to, 4:8] = geo_blocks[wanted(to, 1)]
        send(geo_stage.at[to], geo_got.at[me], 1, (to_grp, to_dev))

    @pl.loop(1, devices)
    def _(step):
        to_grp, to_dev = partner_of(step)
        to = to_grp * members + to_dev
        mode_stage[2 * to] = mode_blocks[wanted(to, 0)]
        mode_stage[2 * to + 1] = mode_blocks[wanted(to, 1)]
        send(mode_stage.at[pl.ds(2 * to, 2)], mode_got.at[pl.ds(2 * me, 2)], 2, (to_grp, to_dev))

    geo_got[me, 0:4] = geo_blocks[wanted(me, 0)]
    geo_got[me, 4:8] = geo_blocks[wanted(me, 1)]
    mode_got[2 * me] = mode_blocks[wanted(me, 0)]
    mode_got[2 * me + 1] = mode_blocks[wanted(me, 1)]
    geos = drain(geo_stage.at[pl.ds(0, others)], geo_got.at[pl.ds(0, others)], 1)
    geos.wait_recv()

    one = jnp.ones((1, P_SIZE), jnp.bfloat16)
    rest = jnp.zeros((KEY - 6, P_SIZE), jnp.bfloat16)
    pad = jnp.zeros((KEY - 12, P_SIZE), jnp.bfloat16)

    @pl.loop(0, devices)
    def _(source):
        block = geo_got[source]
        for rank in range(2):
            slot = 2 * source + rank
            xyz = block[4 * rank : 4 * rank + 3] * FOUR_PI
            area = block[4 * rank + 3 : 4 * rank + 4] * (FOUR_PI * FOUR_PI)
            high, low = split_two(xyz)
            high32, low32 = high.astype(jnp.float32), low.astype(jnp.float32)
            twice_high = (high32 * -2.0).astype(jnp.bfloat16)
            twice_low = (low32 * -2.0).astype(jnp.bfloat16)
            left_xyz[slot] = jnp.concatenate([twice_high, twice_high, twice_low, twice_low, pad], axis=0)
            right_xyz[slot] = jnp.concatenate([high, low, high, low, pad], axis=0)
            whole = high32 + low32
            square = whole * whole
            norm = square[0:1] + square[1:2] + square[2:3]
            for kind, factor in enumerate((1.0, 0.1)):
                a, b, c = split_three(norm + area * factor)
                left_norm[kind * 2 * devices + slot] = jnp.concatenate([a, b, c, one, one, one, rest], axis=0)
                right_norm[kind * 2 * devices + slot] = jnp.concatenate([one, one, one, a, b, c, rest], axis=0)

    gots = drain(mode_stage.at[pl.ds(0, 2 * others)], mode_got.at[pl.ds(0, 2 * others)], 2)
    gots.wait_recv()

    def product(slot):
        code = code_ref[slot]
        other = (code >> 6) & 255
        kind = ((code >> 14) & 1) * (2 * devices)
        keep = ((code >> 15) & 1).astype(jnp.float32)
        left = jnp.concatenate([left_xyz[other], left_norm[kind + other]], axis=0)
        right = jnp.concatenate([right_xyz[slot], right_norm[kind + slot]], axis=0)
        squared = lax.dot_general(
            left, right, (((0,), (0,)), ((), ())), preferred_element_type=jnp.float32
        )
        tile = lax.rsqrt(squared).astype(jnp.bfloat16)
        out = jnp.dot(mode_got[other], tile, preferred_element_type=jnp.float32)
        mode_back[slot] = (out * keep).astype(jnp.bfloat16)

    @pl.loop(1, devices)
    def _(step):
        to_grp, to_dev = partner_of(step)
        to = to_grp * members + to_dev
        product(2 * to)
        product(2 * to + 1)
        send(mode_back.at[pl.ds(2 * to, 2)], back_ref.at[pl.ds(2 * me, 2)], 3, (to_grp, to_dev))

    product(2 * me)
    product(2 * me + 1)
    own = pltpu.make_async_copy(
        mode_back.at[pl.ds(2 * me, 2)], back_ref.at[pl.ds(2 * me, 2)], local_sem
    )
    own.start()
    own.wait()
    backs = drain(mode_back.at[pl.ds(0, 2 * others)], back_ref.at[pl.ds(0, 2 * others)], 3)
    backs.wait_recv()
    requests.wait_send()
    geos.wait_send()
    gots.wait_send()
    backs.wait_send()


def sum_kernel(group, asked_ref, back_ref, out_ref):
    step = pl.program_id(0)

    @pl.when(step == 0)
    def _():
        out_ref[...] = jnp.zeros_like(out_ref)

    for index in range(group):
        slot = step * group + index
        cluster = asked_ref[slot // 2, 0, slot % 2] & 63
        place = pl.ds(pl.multiple_of(cluster * P_SIZE, P_SIZE), P_SIZE)
        out_ref[:, place] += back_ref[index].astype(jnp.float32)


def local(modes, geometry, pair_list, pair_kind):
    groups = lax.axis_size("grp")
    members = lax.axis_size("dev")
    devices = groups * members
    side = math.isqrt(members)
    local_count = modes.shape[1] // P_SIZE
    slots = pair_list.shape[0]
    ends = 2 * slots

    end_ids = pair_list.reshape(ends)
    holder = end_ids // local_count
    order = jnp.arange(ends, dtype=jnp.int32)
    earlier = (holder[:, None] == holder[None, :]) & (order[None, :] < order[:, None])
    place = 2 * holder + jnp.any(earlier, axis=1).astype(jnp.int32)
    other = place.reshape(slots, 2)[:, ::-1].reshape(ends)
    live = pair_kind > 0
    keep = jnp.stack([live, live & (pair_list[:, 0] != pair_list[:, 1])], axis=1).reshape(ends)
    admissible = jnp.repeat(pair_kind == 2, 2)
    code = (
        end_ids % local_count
        + 64 * other
        + 16384 * admissible.astype(jnp.int32)
        + 32768 * keep.astype(jnp.int32)
    )
    code = jnp.sum(jnp.where(place[:, None] == order[None, :], code[:, None], 0), axis=0)
    request = jnp.pad(code.reshape(devices, 1, 2), ((0, 0), (0, 0), (0, 126)))

    vmem = pl.BlockSpec(memory_space=pltpu.VMEM)
    back, asked = pl.pallas_call(
        functools.partial(exchange_kernel, groups, members, side),
        out_shape=[
            jax.ShapeDtypeStruct((ends, MODES, P_SIZE), jnp.bfloat16),
            jax.ShapeDtypeStruct((devices, 1, 128), jnp.int32),
        ],
        in_specs=[pl.BlockSpec(memory_space=pltpu.SMEM), vmem, vmem, vmem],
        out_specs=[pl.BlockSpec(memory_space=pl.ANY), vmem],
        scratch_shapes=[
            pltpu.SMEM((devices, 1, 128), jnp.int32),
            pltpu.VMEM((local_count, MODES, P_SIZE), jnp.bfloat16),
            pltpu.VMEM((local_count, 4, P_SIZE), jnp.float32),
            pltpu.VMEM((devices, 8, P_SIZE), jnp.float32),
            pltpu.VMEM((devices, 8, P_SIZE), jnp.float32),
            pltpu.VMEM((ends, MODES, P_SIZE), jnp.bfloat16),
            pltpu.VMEM((ends, MODES, P_SIZE), jnp.bfloat16),
            pltpu.VMEM((ends, MODES, P_SIZE), jnp.bfloat16),
            pltpu.VMEM((ends, KEY, P_SIZE), jnp.bfloat16),
            pltpu.VMEM((ends, KEY, P_SIZE), jnp.bfloat16),
            pltpu.VMEM((2 * ends, KEY, P_SIZE), jnp.bfloat16),
            pltpu.VMEM((2 * ends, KEY, P_SIZE), jnp.bfloat16),
            pltpu.SemaphoreType.DMA((4,)),
            pltpu.SemaphoreType.DMA((4,)),
            pltpu.SemaphoreType.DMA,
        ],
        compiler_params=pltpu.CompilerParams(
            collective_id=0, has_side_effects=True, vmem_limit_bytes=48 * 1024 * 1024
        ),
    )(code, request, modes, geometry)

    group = 16
    return pl.pallas_call(
        functools.partial(sum_kernel, group),
        grid=(ends // group,),
        out_shape=jax.ShapeDtypeStruct((MODES, local_count * P_SIZE), jnp.float32),
        in_specs=[
            pl.BlockSpec(memory_space=pltpu.SMEM),
            pl.BlockSpec((group, MODES, P_SIZE), lambda step: (step, 0, 0)),
        ],
        out_specs=pl.BlockSpec((MODES, local_count * P_SIZE), lambda step: (0, 0)),
        compiler_params=pltpu.CompilerParams(vmem_limit_bytes=24 * 1024 * 1024),
    )(asked, back)


def solution(mesh):
    placed = (
        P(None, ("grp", "dev")),
        P(None, ("grp", "dev")),
        P(("grp", "dev"), None),
        P(("grp", "dev")),
    )
    return jax.shard_map(
        local, mesh=mesh, in_specs=placed, out_specs=P(None, ("grp", "dev")), check_vma=False
    )
```

```python
import functools
import math

import jax
import jax.numpy as jnp
from jax import lax
from jax.experimental import pallas as pl
from jax.experimental.pallas import tpu as pltpu
from jax.sharding import PartitionSpec as P

P_SIZE = 256
MODES = 32
FOUR_PI = 4.0 * math.pi
MESH = pl.DeviceIdType.MESH


def thirds(value):
    high = value.astype(jnp.bfloat16).astype(jnp.float32)
    rest = value - high
    mid = rest.astype(jnp.bfloat16).astype(jnp.float32)
    return high, mid, rest - mid


def column(row):
    count = row.shape[1]
    down = lax.broadcasted_iota(jnp.int32, (count, count), 0)
    across = lax.broadcasted_iota(jnp.int32, (count, count), 1)
    return jnp.sum(jnp.where(down == across, row, 0), axis=1, keepdims=True)


def slot_table(pair_ids, kinds, local_count):
    slots = pair_ids.shape[1]
    ends = 2 * slots
    left, right = pair_ids[0:1], pair_ids[1:2]
    ids = jnp.concatenate([left, right], axis=1)
    holder = lax.div(ids, local_count)
    down = lax.broadcasted_iota(jnp.int32, (ends, ends), 0)
    across = lax.broadcasted_iota(jnp.int32, (ends, ends), 1)
    earlier = (column(holder) == holder) & (down < across)
    rank = jnp.sum(jnp.where(earlier, 1, 0), axis=0, keepdims=True)
    place = 2 * holder + rank
    other = jnp.concatenate([place[:, slots:], place[:, :slots]], axis=1)
    live = jnp.where(kinds > 0, 1, 0)
    twice = jnp.where(left != right, live, 0)
    keep = jnp.concatenate([live, twice], axis=1)
    admissible = jnp.where(kinds == 2, 1, 0)
    admissible = jnp.concatenate([admissible, admissible], axis=1)
    code = lax.rem(ids, local_count) + 64 * other + 16384 * admissible + 32768 * keep
    return jnp.sum(jnp.where(column(place) == across, column(code), 0), axis=0, keepdims=True)


def exchange_kernel(
    groups, members, side, ahead,
    pair_ref, kind_ref, modes_ref, geo_ref,
    back_ref, wanted_ref,
    code_vmem, code_smem, asked_vmem, asked_smem,
    mode_blocks, geo_blocks, geo_stage, geo_got, mode_stage, mode_got, mode_back, tiles,
    send_sems, recv_sems, local_sem,
):
    devices = groups * members
    others = devices - 1
    local_count = mode_blocks.shape[0]
    grp = lax.axis_index("grp")
    dev = lax.axis_index("dev")
    me = grp * members + dev
    member_bits = members.bit_length() - 1
    side_bits = side.bit_length() - 1

    def partner_of(step):
        shift = (step * 45) & (devices - 1)
        dg, dv = shift >> member_bits, shift & (members - 1)
        y = ((grp >> 1) + (dg >> 1)) & (groups // 2 - 1)
        core = (grp + dg) & 1
        x = ((dev >> side_bits) + (dv >> side_bits)) & (side - 1)
        z = (dev + dv) & (side - 1)
        return y * 2 + core, x * side + z

    barrier = pltpu.get_barrier_semaphore()

    @pl.loop(1, devices)
    def _(step):
        pl.semaphore_signal(barrier, inc=1, device_id=partner_of(step), device_id_type=MESH)

    code_vmem[...] = slot_table(pair_ref[...], kind_ref[...], local_count)
    local = pltpu.make_async_copy(code_vmem, code_smem, local_sem)
    local.start()
    for cluster in range(local_count):
        mode_blocks[cluster] = modes_ref[:, cluster * P_SIZE : (cluster + 1) * P_SIZE]
        geo_blocks[cluster] = geo_ref[:, cluster * P_SIZE : (cluster + 1) * P_SIZE]
    local.wait()

    pl.semaphore_wait(barrier, others)

    def send(source, target, which, place):
        pltpu.make_async_remote_copy(
            src_ref=source, dst_ref=target,
            send_sem=send_sems.at[which], recv_sem=recv_sems.at[which],
            device_id=place, device_id_type=MESH,
        ).start()

    def drain(source, target, which):
        return pltpu.make_async_remote_copy(
            src_ref=source, dst_ref=target,
            send_sem=send_sems.at[which], recv_sem=recv_sems.at[which],
            device_id=(grp, dev), device_id_type=MESH,
        )

    @pl.loop(1, devices)
    def _(step):
        send(code_vmem, asked_vmem.at[me], 0, partner_of(step))

    asked_vmem[me] = code_vmem[...]
    requests = drain(asked_vmem.at[pl.ds(0, others)], asked_vmem.at[pl.ds(0, others)], 0)
    requests.wait_recv()
    local = pltpu.make_async_copy(asked_vmem, asked_smem, local_sem)
    local.start()
    local.wait()

    def wanted(to, rank):
        return asked_smem[to, 0, 2 * me + rank] & 63

    @pl.loop(1, devices)
    def _(step):
        to_grp, to_dev = partner_of(step)
        to = to_grp * members + to_dev
        for rank in range(2):
            cluster = wanted(to, rank)
            wanted_ref[2 * to + rank] = cluster
            geo_stage[to, 4 * rank : 4 * rank + 4] = geo_blocks[cluster]
        send(geo_stage.at[to], geo_got.at[me], 1, (to_grp, to_dev))

    @pl.loop(1, devices)
    def _(step):
        to_grp, to_dev = partner_of(step)
        to = to_grp * members + to_dev
        for rank in range(2):
            mode_stage[2 * to + rank] = mode_blocks[wanted(to, rank)]
        send(mode_stage.at[pl.ds(2 * to, 2)], mode_got.at[pl.ds(2 * me, 2)], 2, (to_grp, to_dev))

    for rank in range(2):
        cluster = wanted(me, rank)
        wanted_ref[2 * me + rank] = cluster
        geo_got[me, 4 * rank : 4 * rank + 4] = geo_blocks[cluster]
        mode_got[2 * me + rank] = mode_blocks[cluster]
    geos = drain(geo_stage.at[pl.ds(0, others)], geo_got.at[pl.ds(0, others)], 1)
    geos.wait_recv()

    row = lax.broadcasted_iota(jnp.int32, (8, P_SIZE), 0)
    scale = jnp.where(row < 3, FOUR_PI, FOUR_PI * FOUR_PI)

    def prepared(block, factor):
        block = block * scale
        square = block * block
        norm = square[0:1] + square[1:2] + square[2:3] + block[3:4] * factor
        return block, norm

    def tile_of(to, rank):
        code = code_smem[0, 2 * to + rank]
        other = (code >> 6) & 255
        factor = jnp.where((code & 16384) != 0, jnp.float32(0.1), jnp.float32(1.0))
        mine = geo_got[to]
        theirs = geo_got[other >> 1]
        if rank == 1:
            mine = pltpu.roll(mine, 4, 0)
        theirs = jnp.where((other & 1) == 1, pltpu.roll(theirs, 4, 0), theirs)
        block, norm = prepared(mine, factor)
        right = jnp.where(row < 3, block, jnp.where(row == 3, norm, jnp.where(row == 4, 1.0, 0.0)))
        block, norm = prepared(theirs, factor)
        left = jnp.where(
            row < 3, -2.0 * block, jnp.where(row == 3, 1.0, jnp.where(row == 4, norm, 0.0))
        )
        a, b, c = thirds(left)
        left = jnp.concatenate([a, b, a, b, c, a], axis=0).astype(jnp.bfloat16)
        a, b, c = thirds(right)
        right = jnp.concatenate([a, a, b, b, a, c], axis=0).astype(jnp.bfloat16)
        squared = lax.dot_general(
            left, right, (((0,), (0,)), ((), ())), preferred_element_type=jnp.float32
        )
        return lax.rsqrt(squared).astype(jnp.bfloat16)

    @pl.loop(1, ahead)
    def _(step):
        to_grp, to_dev = partner_of(step)
        to = to_grp * members + to_dev
        for rank in range(2):
            tiles[2 * step + rank] = tile_of(to, rank)

    gots = drain(mode_stage.at[pl.ds(0, 2 * others)], mode_got.at[pl.ds(0, 2 * others)], 2)
    gots.wait_recv()

    def product(to, rank, tile):
        code = code_smem[0, 2 * to + rank]
        keep = ((code >> 15) & 1).astype(jnp.float32)
        out = jnp.dot(mode_got[(code >> 6) & 255], tile, preferred_element_type=jnp.float32)
        mode_back[2 * to + rank] = (out * keep).astype(jnp.bfloat16)

    def give_back(to, place):
        send(mode_back.at[pl.ds(2 * to, 2)], back_ref.at[pl.ds(2 * me, 2)], 3, place)

    @pl.loop(1, ahead)
    def _(step):
        to_grp, to_dev = partner_of(step)
        to = to_grp * members + to_dev
        for rank in range(2):
            product(to, rank, tiles[2 * step + rank])
        give_back(to, (to_grp, to_dev))

    @pl.loop(ahead, devices)
    def _(step):
        to_grp, to_dev = partner_of(step)
        to = to_grp * members + to_dev
        for rank in range(2):
            product(to, rank, tile_of(to, rank))
        give_back(to, (to_grp, to_dev))

    for rank in range(2):
        product(me, rank, tile_of(me, rank))
    own = pltpu.make_async_copy(
        mode_back.at[pl.ds(2 * me, 2)], back_ref.at[pl.ds(2 * me, 2)], local_sem
    )
    own.start()
    own.wait()
    backs = drain(mode_back.at[pl.ds(0, 2 * others)], back_ref.at[pl.ds(0, 2 * others)], 3)
    backs.wait_recv()
    requests.wait_send()
    geos.wait_send()
    gots.wait_send()
    backs.wait_send()


def sum_kernel(group, wanted_ref, back_ref, out_ref):
    step = pl.program_id(0)

    @pl.when(step == 0)
    def _():
        out_ref[...] = jnp.zeros_like(out_ref)

    for index in range(group):
        cluster = wanted_ref[step * group + index]
        place = pl.ds(pl.multiple_of(cluster * P_SIZE, P_SIZE), P_SIZE)
        out_ref[:, place] += back_ref[index].astype(jnp.float32)


def local(modes, geometry, pair_list, pair_kind):
    groups = lax.axis_size("grp")
    members = lax.axis_size("dev")
    devices = groups * members
    side = math.isqrt(members)
    local_count = modes.shape[1] // P_SIZE
    slots = pair_list.shape[0]
    ends = 2 * slots
    ahead = devices * 3 // 4

    vmem = pl.BlockSpec(memory_space=pltpu.VMEM)
    smem = pl.BlockSpec(memory_space=pltpu.SMEM)
    back, wanted = pl.pallas_call(
        functools.partial(exchange_kernel, groups, members, side, ahead),
        out_shape=[
            jax.ShapeDtypeStruct((ends, MODES, P_SIZE), jnp.bfloat16),
            jax.ShapeDtypeStruct((ends,), jnp.int32),
        ],
        in_specs=[vmem, vmem, vmem, vmem],
        out_specs=[pl.BlockSpec(memory_space=pl.ANY), smem],
        scratch_shapes=[
            pltpu.VMEM((1, ends), jnp.int32),
            pltpu.SMEM((1, ends), jnp.int32),
            pltpu.VMEM((devices, 1, ends), jnp.int32),
            pltpu.SMEM((devices, 1, ends), jnp.int32),
            pltpu.VMEM((local_count, MODES, P_SIZE), jnp.bfloat16),
            pltpu.VMEM((local_count, 4, P_SIZE), jnp.float32),
            pltpu.VMEM((devices, 8, P_SIZE), jnp.float32),
            pltpu.VMEM((devices, 8, P_SIZE), jnp.float32),
            pltpu.VMEM((ends, MODES, P_SIZE), jnp.bfloat16),
            pltpu.VMEM((ends, MODES, P_SIZE), jnp.bfloat16),
            pltpu.VMEM((ends, MODES, P_SIZE), jnp.bfloat16),
            pltpu.VMEM((2 * ahead, P_SIZE, P_SIZE), jnp.bfloat16),
            pltpu.SemaphoreType.DMA((4,)),
            pltpu.SemaphoreType.DMA((4,)),
            pltpu.SemaphoreType.DMA,
        ],
        compiler_params=pltpu.CompilerParams(
            collective_id=0, has_side_effects=True, vmem_limit_bytes=56 * 1024 * 1024
        ),
    )(pair_list.T, pair_kind.reshape(1, slots), modes, geometry)

    group = 16
    return pl.pallas_call(
        functools.partial(sum_kernel, group),
        grid=(ends // group,),
        out_shape=jax.ShapeDtypeStruct((MODES, local_count * P_SIZE), jnp.float32),
        in_specs=[
            smem,
            pl.BlockSpec((group, MODES, P_SIZE), lambda step: (step, 0, 0)),
        ],
        out_specs=pl.BlockSpec((MODES, local_count * P_SIZE), lambda step: (0, 0)),
        compiler_params=pltpu.CompilerParams(vmem_limit_bytes=24 * 1024 * 1024),
    )(wanted, back)


def solution(mesh):
    placed = (
        P(None, ("grp", "dev")),
        P(None, ("grp", "dev")),
        P(("grp", "dev"), None),
        P(("grp", "dev")),
    )
    return jax.shard_map(
        local, mesh=mesh, in_specs=placed, out_specs=P(None, ("grp", "dev")), check_vma=False
    )
```

```python
import functools
import math

import jax
import jax.numpy as jnp
from jax import lax
from jax.experimental import pallas as pl
from jax.experimental.pallas import tpu as pltpu
from jax.sharding import PartitionSpec as P

P_SIZE = 256
HALF = 16
X_STEPS = 32767.0 / 2.4
A_STEPS = 32767.0 / 2.0
FOUR_PI = 4.0 * math.pi
MESH = pl.DeviceIdType.MESH


def thirds(value):
    high = value.astype(jnp.bfloat16).astype(jnp.float32)
    rest = value - high
    mid = rest.astype(jnp.bfloat16).astype(jnp.float32)
    return high, mid, rest - mid


def column(row):
    count = row.shape[1]
    down = lax.broadcasted_iota(jnp.int32, (count, count), 0)
    across = lax.broadcasted_iota(jnp.int32, (count, count), 1)
    return jnp.sum(jnp.where(down == across, row, 0), axis=1, keepdims=True)


def slot_table(pair_ids, kinds, local_count):
    slots = pair_ids.shape[1]
    ends = 2 * slots
    left, right = pair_ids[0:1], pair_ids[1:2]
    ids = jnp.concatenate([left, right], axis=1)
    holder = lax.div(ids, local_count)
    down = lax.broadcasted_iota(jnp.int32, (ends, ends), 0)
    across = lax.broadcasted_iota(jnp.int32, (ends, ends), 1)
    holder_down = column(holder)
    same = holder_down == holder
    rank = jnp.sum(jnp.where(same & (down < across), 1, 0), axis=0, keepdims=True)
    rank_down = jnp.sum(jnp.where(same & (across < down), 1, 0), axis=1, keepdims=True)
    place = 2 * holder + rank
    other = jnp.concatenate([place[:, slots:], place[:, :slots]], axis=1)
    live = jnp.where(kinds > 0, 1, 0)
    twice = jnp.where(left != right, live, 0)
    keep = jnp.concatenate([live, twice], axis=1)
    admissible = jnp.where(kinds == 2, 1, 0)
    admissible = jnp.concatenate([admissible, admissible], axis=1)
    code = lax.rem(ids, local_count) + 64 * other + 16384 * admissible + 32768 * keep
    code_down = column(code)
    place_down = 2 * holder_down + rank_down
    table = jnp.sum(jnp.where(place_down == across, code_down, 0), axis=0, keepdims=True)
    asked = (code_down & 63) * (1 + 63 * rank_down)
    lanes = lax.broadcasted_iota(jnp.int32, (ends, 128), 1)
    request = jnp.sum(jnp.where(holder_down == lanes, asked, 0), axis=0, keepdims=True)
    return table, request


def exchange_kernel(
    groups, members, side,
    pair_ref, kind_ref, modes_ref, geo_ref,
    back_ref, wanted_ref,
    code_vmem, code_smem, row_vmem, asked_vmem, asked_smem,
    mode_blocks, geo_blocks, geo_stage, geo_got,
    mode_stage, first_got, second_got, mode_back, tiles,
    send_sems, recv_sems, local_sem,
):
    devices = groups * members
    others = devices - 1
    local_count = geo_blocks.shape[0]
    grp = lax.axis_index("grp")
    dev = lax.axis_index("dev")
    me = grp * members + dev
    member_bits = members.bit_length() - 1
    side_bits = side.bit_length() - 1

    def partner_of(step):
        shift = (step * 45) & (devices - 1)
        dg, dv = shift >> member_bits, shift & (members - 1)
        y = ((grp >> 1) + (dg >> 1)) & (groups // 2 - 1)
        core = (grp + dg) & 1
        x = ((dev >> side_bits) + (dv >> side_bits)) & (side - 1)
        z = (dev + dv) & (side - 1)
        return y * 2 + core, x * side + z

    def in_row(shift):
        return grp, (dev + shift) & (members - 1)

    def in_column(shift):
        return (grp + shift) & (groups - 1), dev

    def two_steps(passes, body):
        @pl.loop(0, passes)
        def _(index):
            for step in (2 * index + 1, 2 * index + 2):
                place = partner_of(step)
                body(step, place, place[0] * members + place[1])

    def send(source, target, which, place):
        pltpu.make_async_remote_copy(
            src_ref=source, dst_ref=target,
            send_sem=send_sems.at[which], recv_sem=recv_sems.at[which],
            device_id=place, device_id_type=MESH,
        ).start()

    def drain(source, target, which):
        return pltpu.make_async_remote_copy(
            src_ref=source, dst_ref=target,
            send_sem=send_sems.at[which], recv_sem=recv_sems.at[which],
            device_id=(grp, dev), device_id_type=MESH,
        )

    barrier = pltpu.get_barrier_semaphore()
    for shift in range(1, members):
        pl.semaphore_signal(barrier, inc=1, device_id=in_row(shift), device_id_type=MESH)
    for shift in range(1, groups):
        pl.semaphore_signal(barrier, inc=1, device_id=in_column(shift), device_id_type=MESH)

    table, request = slot_table(pair_ref[...], kind_ref[...], local_count)
    row_vmem[...] = request
    asked_vmem[me] = request
    code_vmem[...] = table
    local = pltpu.make_async_copy(code_vmem, code_smem, local_sem)
    local.start()
    high_rows = lax.broadcasted_iota(jnp.int32, (4, P_SIZE), 0)
    steps = jnp.where(high_rows < 3, X_STEPS, A_STEPS)
    for cluster in range(local_count):
        panels = slice(cluster * P_SIZE, (cluster + 1) * P_SIZE)
        mode_blocks[0, cluster] = modes_ref[0:HALF, panels]
        mode_blocks[1, cluster] = modes_ref[HALF : 2 * HALF, panels]
        geo_blocks[cluster] = jnp.round(geo_ref[:, panels] * steps)
    local.wait()
    pl.semaphore_wait(barrier, members + groups - 2)

    for shift in range(1, members):
        send(row_vmem, asked_vmem.at[me], 0, in_row(shift))
    along_row = drain(asked_vmem.at[pl.ds(0, members - 1)], asked_vmem.at[pl.ds(0, members - 1)], 0)
    along_row.wait_recv()
    for shift in range(1, groups):
        mine = asked_vmem.at[pl.ds(grp * members, members)]
        send(mine, mine, 1, in_column(shift))
    far = asked_vmem.at[pl.ds(0, members * (groups - 1))]
    along_column = drain(far, far, 1)
    along_column.wait_recv()
    local = pltpu.make_async_copy(asked_vmem, asked_smem, local_sem)
    local.start()
    local.wait()

    def wanted(to, rank):
        return (asked_smem[to, 0, me] >> (6 * rank)) & 63

    def geo_for(to):
        both = jnp.concatenate([geo_blocks[wanted(to, 0)], geo_blocks[wanted(to, 1)]], axis=0)
        both = jnp.concatenate([both[:, :128], both[:, 128:]], axis=0)
        return both.astype(jnp.int32).astype(jnp.int16)

    def send_geo(step, place, to):
        geo_stage[to] = geo_for(to)
        send(geo_stage.at[to], geo_got.at[me], 2, place)

    def send_modes(half, got):
        def body(step, place, to):
            for rank in range(2):
                mode_stage[half, 2 * to + rank] = mode_blocks[half, wanted(to, rank)]
            send(
                mode_stage.at[half, pl.ds(2 * to, 2)], got.at[pl.ds(2 * me, 2)], 3 + half, place
            )
        return body

    def all_partners(body):
        two_steps(others // 2, body)
        place = partner_of(others)
        body(others, place, place[0] * members + place[1])

    all_partners(send_geo)
    all_partners(send_modes(0, first_got))
    all_partners(send_modes(1, second_got))
    geo_got[me] = geo_for(me)
    for rank in range(2):
        first_got[2 * me + rank] = mode_blocks[0, wanted(me, rank)]
        second_got[2 * me + rank] = mode_blocks[1, wanted(me, rank)]

    @pl.loop(0, devices)
    def _(to):
        for rank in range(2):
            wanted_ref[2 * to + rank] = wanted(to, rank)

    geos = drain(geo_stage.at[pl.ds(0, others)], geo_got.at[pl.ds(0, others)], 2)
    geos.wait_recv()

    row = lax.broadcasted_iota(jnp.int32, (8, P_SIZE), 0)
    scale = jnp.where(
        (row & 3) < 3, FOUR_PI / X_STEPS, FOUR_PI * FOUR_PI / A_STEPS
    )

    def both_clusters(source):
        block = geo_got[source].astype(jnp.int32).astype(jnp.float32)
        return jnp.concatenate([block[0:8], block[8:16]], axis=1) * scale

    def length(block, factor):
        square = block * block
        return square[0:1] + square[1:2] + square[2:3] + block[3:4] * factor

    def tile_of(to, rank):
        code = code_smem[0, 2 * to + rank]
        other = (code >> 6) & 255
        factor = jnp.where((code & 16384) != 0, jnp.float32(0.1), jnp.float32(1.0))
        mine = both_clusters(to)
        theirs = both_clusters(other >> 1)
        if rank == 1:
            mine = pltpu.roll(mine, 4, 0)
        theirs = jnp.where((other & 1) == 1, pltpu.roll(theirs, 4, 0), theirs)
        norm = length(mine, factor)
        right = jnp.where(row < 3, mine, jnp.where(row == 3, norm, jnp.where(row == 4, 1.0, 0.0)))
        norm = length(theirs, factor)
        left = jnp.where(
            row < 3, -2.0 * theirs, jnp.where(row == 3, 1.0, jnp.where(row == 4, norm, 0.0))
        )
        a, b, c = thirds(left)
        left = jnp.concatenate([a, b, a, b, c, a], axis=0).astype(jnp.bfloat16)
        a, b, c = thirds(right)
        right = jnp.concatenate([a, a, b, b, a, c], axis=0).astype(jnp.bfloat16)
        squared = lax.dot_general(
            left, right, (((0,), (0,)), ((), ())), preferred_element_type=jnp.float32
        )
        return lax.rsqrt(squared).astype(jnp.bfloat16)

    def make_tiles(step, place, to):
        for rank in range(2):
            tiles[2 * (step - 1) + rank] = tile_of(to, rank)

    two_steps(devices // 2, make_tiles)

    def product(half, got, step, to, rank):
        code = code_smem[0, 2 * to + rank]
        keep = ((code >> 15) & 1).astype(jnp.float32)
        out = jnp.dot(
            got[(code >> 6) & 255], tiles[2 * (step - 1) + rank], preferred_element_type=jnp.float32
        )
        mode_back[half, 2 * to + rank] = (out * keep).astype(jnp.bfloat16)

    def return_half(half, got):
        def give_back(to, place):
            send(
                mode_back.at[half, pl.ds(2 * to, 2)], back_ref.at[half, pl.ds(2 * me, 2)],
                5 + half, place,
            )

        def two_products(first, second):
            places = []
            for step in (first, second):
                place = partner_of(step)
                to = place[0] * members + place[1]
                places.append((to, place))
                for rank in range(2):
                    product(half, got, step, to, rank)
            return places

        @pl.loop(0, devices // 2 - 1)
        def _(index):
            for to, place in two_products(2 * index + 1, 2 * index + 2):
                give_back(to, place)

        give_back(*two_products(others, devices)[0])

    gots = []
    for half, got in enumerate((first_got, second_got)):
        arrived = drain(
            mode_stage.at[half, pl.ds(0, 2 * others)], got.at[pl.ds(0, 2 * others)], 3 + half
        )
        arrived.wait_recv()
        gots.append(arrived)
        return_half(half, got)

    for half in range(2):
        own = pltpu.make_async_copy(
            mode_back.at[half, pl.ds(2 * me, 2)], back_ref.at[half, pl.ds(2 * me, 2)], local_sem
        )
        own.start()
        own.wait()
    for half in range(2):
        backs = drain(
            mode_back.at[half, pl.ds(0, 2 * others)], back_ref.at[half, pl.ds(0, 2 * others)],
            5 + half,
        )
        backs.wait_recv()
        backs.wait_send()
    along_row.wait_send()
    along_column.wait_send()
    geos.wait_send()
    for arrived in gots:
        arrived.wait_send()


def sum_kernel(chunks, wanted_ref, back_ref, out_ref, arrived, total, in_sems, out_sems):
    ends = back_ref.shape[1]
    count = ends // chunks

    def piece(half, chunk):
        part = pl.ds(chunk * count, count)
        return pltpu.make_async_copy(
            back_ref.at[half, part], arrived.at[half, part], in_sems.at[half * chunks + chunk]
        )

    for half in range(2):
        for chunk in range(chunks):
            piece(half, chunk).start()
    total[...] = jnp.zeros_like(total)
    written = []
    for half in range(2):
        rows = pl.ds(half * HALF, HALF)
        for chunk in range(chunks):
            piece(half, chunk).wait()

            @pl.loop(0, count, unroll=8)
            def _(index):
                slot = chunk * count + index
                place = pl.ds(pl.multiple_of(wanted_ref[slot] * P_SIZE, P_SIZE), P_SIZE)
                total[rows, place] += arrived[half, slot].astype(jnp.float32)

        written.append(pltpu.make_async_copy(total.at[rows], out_ref.at[rows], out_sems.at[half]))
        written[-1].start()
    for copy in written:
        copy.wait()


def local(modes, geometry, pair_list, pair_kind):
    groups = lax.axis_size("grp")
    members = lax.axis_size("dev")
    devices = groups * members
    side = math.isqrt(members)
    local_count = modes.shape[1] // P_SIZE
    slots = pair_list.shape[0]
    ends = 2 * slots

    vmem = pl.BlockSpec(memory_space=pltpu.VMEM)
    smem = pl.BlockSpec(memory_space=pltpu.SMEM)
    back, wanted = pl.pallas_call(
        functools.partial(exchange_kernel, groups, members, side),
        out_shape=[
            jax.ShapeDtypeStruct((2, ends, HALF, P_SIZE), jnp.bfloat16),
            jax.ShapeDtypeStruct((ends,), jnp.int32),
        ],
        in_specs=[vmem, vmem, vmem, vmem],
        out_specs=[pl.BlockSpec(memory_space=pl.ANY), smem],
        scratch_shapes=[
            pltpu.VMEM((1, ends), jnp.int32),
            pltpu.SMEM((1, ends), jnp.int32),
            pltpu.VMEM((1, 128), jnp.int32),
            pltpu.VMEM((devices, 1, 128), jnp.int32),
            pltpu.SMEM((devices, 1, 128), jnp.int32),
            pltpu.VMEM((2, local_count, HALF, P_SIZE), jnp.bfloat16),
            pltpu.VMEM((local_count, 4, P_SIZE), jnp.float32),
            pltpu.VMEM((devices, 16, 128), jnp.int16),
            pltpu.VMEM((devices, 16, 128), jnp.int16),
            pltpu.VMEM((2, ends, HALF, P_SIZE), jnp.bfloat16),
            pltpu.VMEM((ends, HALF, P_SIZE), jnp.bfloat16),
            pltpu.VMEM((ends, HALF, P_SIZE), jnp.bfloat16),
            pltpu.VMEM((2, ends, HALF, P_SIZE), jnp.bfloat16),
            pltpu.VMEM((ends, P_SIZE, P_SIZE), jnp.bfloat16),
            pltpu.SemaphoreType.DMA((7,)),
            pltpu.SemaphoreType.DMA((7,)),
            pltpu.SemaphoreType.DMA,
        ],
        compiler_params=pltpu.CompilerParams(
            collective_id=0, has_side_effects=True, vmem_limit_bytes=56 * 1024 * 1024
        ),
    )(pair_list.T, pair_kind.reshape(1, slots), modes, geometry)

    chunks = 4
    anywhere = pl.BlockSpec(memory_space=pl.ANY)
    return pl.pallas_call(
        functools.partial(sum_kernel, chunks),
        out_shape=jax.ShapeDtypeStruct((2 * HALF, local_count * P_SIZE), jnp.float32),
        in_specs=[smem, anywhere],
        out_specs=anywhere,
        scratch_shapes=[
            pltpu.VMEM((2, ends, HALF, P_SIZE), jnp.bfloat16),
            pltpu.VMEM((2 * HALF, local_count * P_SIZE), jnp.float32),
            pltpu.SemaphoreType.DMA((2 * chunks,)),
            pltpu.SemaphoreType.DMA((2,)),
        ],
        compiler_params=pltpu.CompilerParams(vmem_limit_bytes=56 * 1024 * 1024),
    )(wanted, back)


def solution(mesh):
    placed = (
        P(None, ("grp", "dev")),
        P(None, ("grp", "dev")),
        P(("grp", "dev"), None),
        P(("grp", "dev")),
    )
    return jax.shard_map(
        local, mesh=mesh, in_specs=placed, out_specs=P(None, ("grp", "dev")), check_vma=False
    )
```

```python
import functools
import math

import jax
import jax.numpy as jnp
from jax import lax
from jax.experimental import pallas as pl
from jax.experimental.pallas import tpu as pltpu
from jax.sharding import PartitionSpec as P

P_SIZE = 256
HALF = 16
X_STEPS = 32767.0 / 2.4
A_STEPS = 32767.0 / 2.0
FOUR_PI = 4.0 * math.pi
MESH = pl.DeviceIdType.MESH


def thirds(value):
    high = value.astype(jnp.bfloat16).astype(jnp.float32)
    rest = value - high
    mid = rest.astype(jnp.bfloat16).astype(jnp.float32)
    return high, mid, rest - mid


def column(row):
    count = row.shape[1]
    down = lax.broadcasted_iota(jnp.int32, (count, count), 0)
    across = lax.broadcasted_iota(jnp.int32, (count, count), 1)
    return jnp.sum(jnp.where(down == across, row, 0), axis=1, keepdims=True)


def slot_table(pair_ids, kinds, local_count):
    slots = pair_ids.shape[1]
    ends = 2 * slots
    left, right = pair_ids[0:1], pair_ids[1:2]
    ids = jnp.concatenate([left, right], axis=1)
    holder = lax.div(ids, local_count)
    down = lax.broadcasted_iota(jnp.int32, (ends, ends), 0)
    across = lax.broadcasted_iota(jnp.int32, (ends, ends), 1)
    holder_down = column(holder)
    same = holder_down == holder
    rank = jnp.sum(jnp.where(same & (down < across), 1, 0), axis=0, keepdims=True)
    rank_down = jnp.sum(jnp.where(same & (across < down), 1, 0), axis=1, keepdims=True)
    place = 2 * holder + rank
    other = jnp.concatenate([place[:, slots:], place[:, :slots]], axis=1)
    live = jnp.where(kinds > 0, 1, 0)
    twice = jnp.where(left != right, live, 0)
    keep = jnp.concatenate([live, twice], axis=1)
    admissible = jnp.where(kinds == 2, 1, 0)
    admissible = jnp.concatenate([admissible, admissible], axis=1)
    code = lax.rem(ids, local_count) + 64 * other + 16384 * admissible + 32768 * keep
    code_down = column(code)
    place_down = 2 * holder_down + rank_down
    table = jnp.sum(jnp.where(place_down == across, code_down, 0), axis=0, keepdims=True)
    asked = (code_down & 63) * (1 + 63 * rank_down)
    lanes = lax.broadcasted_iota(jnp.int32, (ends, 128), 1)
    request = jnp.sum(jnp.where(holder_down == lanes, asked, 0), axis=0, keepdims=True)
    return table, request


def exchange_kernel(
    groups, members, side,
    pair_hbm, kind_hbm, modes_hbm, geo_hbm,
    back_ref, wanted_ref,
    pair_ref, kind_ref, modes_ref, geo_ref,
    code_vmem, code_smem, row_vmem, asked_vmem, asked_smem,
    mode_blocks, geo_blocks, geo_stage, geo_got,
    mode_stage, first_got, second_got, mode_back, tiles,
    send_sems, recv_sems, cell_sems, row_sems, local_sem, input_sems,
):
    devices = groups * members
    others = devices - 1
    local_count = geo_blocks.shape[0]
    grp = lax.axis_index("grp")
    dev = lax.axis_index("dev")
    me = grp * members + dev
    member_bits = members.bit_length() - 1
    side_bits = side.bit_length() - 1

    def partner_of(step):
        shift = (step * 11) & (devices - 1)
        dg, dv = shift >> member_bits, shift & (members - 1)
        y = ((grp >> 1) + (dg >> 1)) & (groups // 2 - 1)
        core = (grp + dg) & 1
        x = ((dev >> side_bits) + (dv >> side_bits)) & (side - 1)
        z = (dev + dv) & (side - 1)
        return y * 2 + core, x * side + z

    cell = devices // 8
    fold = side // 2
    fold_bits = fold.bit_length() - 1
    my_y, my_core, my_x, my_z = grp >> 1, grp & 1, dev >> side_bits, dev & (side - 1)

    def key_of(place):
        y, core, x, z = place[0] >> 1, place[0] & 1, place[1] >> side_bits, place[1] & (side - 1)
        which = (y & 1) * 4 + (x & 1) * 2 + (z & 1)
        return which * cell + (((y >> 1) * fold + (x >> 1)) * fold + (z >> 1)) * 2 + core

    def at(dy, core, dx, dz):
        y = (my_y + dy) & (groups // 2 - 1)
        x, z = (my_x + dx) & (side - 1), (my_z + dz) & (side - 1)
        return y * 2 + ((my_core + core) & 1), x * side + z

    def in_cell(which, index):
        z = (index >> 1) & (fold - 1)
        x = (index >> (1 + fold_bits)) & (fold - 1)
        y = index >> (1 + 2 * fold_bits)
        return at(
            ((which >> 2) & 1) + 2 * y, index & 1, ((which >> 1) & 1) + 2 * x, (which & 1) + 2 * z
        )

    my_key = key_of((grp, dev))
    my_rows = pl.ds(my_key // cell * cell, cell)

    def two_steps(passes, body):
        @pl.loop(0, passes)
        def _(index):
            for step in (2 * index + 1, 2 * index + 2):
                place = partner_of(step)
                body(step, place, place[0] * members + place[1])

    def send(source, target, which, place):
        pltpu.make_async_remote_copy(
            src_ref=source, dst_ref=target,
            send_sem=send_sems.at[which], recv_sem=recv_sems.at[which],
            device_id=place, device_id_type=MESH,
        ).start()

    def drain(source, target, which):
        return pltpu.make_async_remote_copy(
            src_ref=source, dst_ref=target,
            send_sem=send_sems.at[which], recv_sem=recv_sems.at[which],
            device_id=(grp, dev), device_id_type=MESH,
        )

    barrier = pltpu.get_barrier_semaphore()
    for index in range(1, cell):
        pl.semaphore_signal(barrier, inc=1, device_id=in_cell(0, index), device_id_type=MESH)
    for which in range(1, 8):
        source = at(-(which >> 2), 0, -((which >> 1) & 1), -(which & 1))
        pl.semaphore_signal(barrier, inc=1, device_id=source, device_id_type=MESH)

    inputs = [
        pltpu.make_async_copy(source, target, input_sems.at[index])
        for index, (source, target) in enumerate((
            (pair_hbm, pair_ref), (kind_hbm, kind_ref), (geo_hbm, geo_ref), (modes_hbm, modes_ref),
        ))
    ]
    for copy in inputs:
        copy.start()
    inputs[0].wait()
    inputs[1].wait()
    table, request = slot_table(pair_ref[...], kind_ref[...], local_count)
    row_vmem[...] = request
    asked_vmem[my_key] = request
    code_vmem[...] = table
    local = pltpu.make_async_copy(code_vmem, code_smem, local_sem)
    local.start()
    high_rows = lax.broadcasted_iota(jnp.int32, (4, P_SIZE), 0)
    steps = jnp.where(high_rows < 3, X_STEPS, A_STEPS)
    inputs[2].wait()
    inputs[3].wait()
    for cluster in range(local_count):
        panels = slice(cluster * P_SIZE, (cluster + 1) * P_SIZE)
        mode_blocks[0, cluster] = modes_ref[0:HALF, panels]
        mode_blocks[1, cluster] = modes_ref[HALF : 2 * HALF, panels]
        geo_blocks[cluster] = jnp.round(geo_ref[:, panels] * steps)
    local.wait()
    pl.semaphore_wait(barrier, cell + 6)

    for index in range(1, cell):
        send(row_vmem, asked_vmem.at[my_key], 0, in_cell(0, index))
    in_own = drain(asked_vmem.at[pl.ds(0, cell - 1)], asked_vmem.at[pl.ds(0, cell - 1)], 0)
    in_own.wait_recv()

    def across(which):
        return pltpu.make_async_remote_copy(
            src_ref=asked_vmem.at[my_rows], dst_ref=asked_vmem.at[my_rows],
            send_sem=send_sems.at[1], recv_sem=cell_sems.at[which],
            device_id=in_cell(which, 0), device_id_type=MESH,
        )

    def readable(which):
        rows = pl.ds(key_of(in_cell(which, 0)) // cell * cell, cell)
        return pltpu.make_async_copy(asked_vmem.at[rows], asked_smem.at[rows], row_sems.at[which])

    for which in range(1, 8):
        across(which).start()
    local = readable(0)
    local.start()
    local.wait()

    def wanted(to, rank):
        place = (to >> member_bits, to & (members - 1))
        return (asked_smem[key_of(place), 0, me] >> (6 * rank)) & 63

    def geo_for(to):
        both = jnp.concatenate([geo_blocks[wanted(to, 0)], geo_blocks[wanted(to, 1)]], axis=0)
        both = jnp.concatenate([both[:, :128], both[:, 128:]], axis=0)
        return both.astype(jnp.int32).astype(jnp.int16)

    def send_geo(step, place, to):
        geo_stage[to] = geo_for(to)
        send(geo_stage.at[to], geo_got.at[me], 2, place)

    def send_modes(half, got):
        def body(step, place, to):
            for rank in range(2):
                mode_stage[half, 2 * to + rank] = mode_blocks[half, wanted(to, rank)]
            send(
                mode_stage.at[half, pl.ds(2 * to, 2)], got.at[pl.ds(2 * me, 2)], 3 + half, place
            )
        return body

    def at_place(place, body):
        body(0, place, place[0] * members + place[1])

    send_first = send_modes(0, first_got)
    send_second = send_modes(1, second_got)

    for body in (send_geo, send_first, send_second):
        @pl.loop(1, cell)
        def _(index):
            at_place(in_cell(0, index), body)

    def geos_for(which):
        readable(which).wait()

        @pl.loop(0, cell // 2)
        def _(index):
            at_place(in_cell(which, 2 * index), send_geo)
            at_place(in_cell(which, 2 * index + 1), send_geo)

    across(1).wait_recv()
    readable(1).start()

    @pl.loop(1, 7)
    def _(which):
        across(which + 1).wait_recv()
        readable(which + 1).start()
        geos_for(which)

    geos_for(7)

    away = 7 * cell
    for body in (send_first, send_second):
        @pl.loop(0, away // 2)
        def _(index):
            for step in (2 * index, 2 * index + 1):
                turn = lax.rem(step * 11, away)
                at_place(in_cell(1 + (turn >> (cell.bit_length() - 1)), turn & (cell - 1)), body)

    geo_got[me] = geo_for(me)
    for rank in range(2):
        first_got[2 * me + rank] = mode_blocks[0, wanted(me, rank)]
        second_got[2 * me + rank] = mode_blocks[1, wanted(me, rank)]

    @pl.loop(0, devices)
    def _(to):
        for rank in range(2):
            wanted_ref[2 * to + rank] = wanted(to, rank)

    geos = drain(geo_stage.at[pl.ds(0, others)], geo_got.at[pl.ds(0, others)], 2)
    geos.wait_recv()

    row = lax.broadcasted_iota(jnp.int32, (8, P_SIZE), 0)
    scale = jnp.where(
        (row & 3) < 3, FOUR_PI / X_STEPS, FOUR_PI * FOUR_PI / A_STEPS
    )

    def both_clusters(source):
        block = geo_got[source].astype(jnp.int32).astype(jnp.float32)
        return jnp.concatenate([block[0:8], block[8:16]], axis=1) * scale

    def length(block, factor):
        square = block * block
        return square[0:1] + square[1:2] + square[2:3] + block[3:4] * factor

    def tile_of(to, rank):
        code = code_smem[0, 2 * to + rank]
        other = (code >> 6) & 255
        factor = jnp.where((code & 16384) != 0, jnp.float32(0.1), jnp.float32(1.0))
        mine = both_clusters(to)
        theirs = both_clusters(other >> 1)
        if rank == 1:
            mine = pltpu.roll(mine, 4, 0)
        theirs = jnp.where((other & 1) == 1, pltpu.roll(theirs, 4, 0), theirs)
        norm = length(mine, factor)
        right = jnp.where(row < 3, mine, jnp.where(row == 3, norm, jnp.where(row == 4, 1.0, 0.0)))
        norm = length(theirs, factor)
        left = jnp.where(
            row < 3, -2.0 * theirs, jnp.where(row == 3, 1.0, jnp.where(row == 4, norm, 0.0))
        )
        a, b, c = thirds(left)
        left = jnp.concatenate([a, b, a, b, c, a], axis=0).astype(jnp.bfloat16)
        a, b, c = thirds(right)
        right = jnp.concatenate([a, a, b, b, a, c], axis=0).astype(jnp.bfloat16)
        squared = lax.dot_general(
            left, right, (((0,), (0,)), ((), ())), preferred_element_type=jnp.float32
        )
        return lax.rsqrt(squared).astype(jnp.bfloat16)

    def make_tiles(step, place, to):
        for rank in range(2):
            tiles[2 * (step - 1) + rank] = tile_of(to, rank)

    two_steps(devices // 2, make_tiles)

    def product(half, got, step, to, rank):
        code = code_smem[0, 2 * to + rank]
        keep = ((code >> 15) & 1).astype(jnp.float32)
        out = jnp.dot(
            got[(code >> 6) & 255], tiles[2 * (step - 1) + rank], preferred_element_type=jnp.float32
        )
        mode_back[half, 2 * to + rank] = (out * keep).astype(jnp.bfloat16)

    def return_half(half, got):
        def give_back(to, place):
            send(
                mode_back.at[half, pl.ds(2 * to, 2)], back_ref.at[half, pl.ds(2 * me, 2)],
                5 + half, place,
            )

        def two_products(first, second):
            places = []
            for step in (first, second):
                place = partner_of(step)
                to = place[0] * members + place[1]
                places.append((to, place))
                for rank in range(2):
                    product(half, got, step, to, rank)
            return places

        @pl.loop(0, devices // 2 - 1)
        def _(index):
            for to, place in two_products(2 * index + 1, 2 * index + 2):
                give_back(to, place)

        give_back(*two_products(others, devices)[0])

    gots = []
    for half, got in enumerate((first_got, second_got)):
        arrived = drain(
            mode_stage.at[half, pl.ds(0, 2 * others)], got.at[pl.ds(0, 2 * others)], 3 + half
        )
        arrived.wait_recv()
        gots.append(arrived)
        return_half(half, got)

    for half in range(2):
        own = pltpu.make_async_copy(
            mode_back.at[half, pl.ds(2 * me, 2)], back_ref.at[half, pl.ds(2 * me, 2)], local_sem
        )
        own.start()
        own.wait()
    for half in range(2):
        backs = drain(
            mode_back.at[half, pl.ds(0, 2 * others)], back_ref.at[half, pl.ds(0, 2 * others)],
            5 + half,
        )
        backs.wait_recv()
        backs.wait_send()
    in_own.wait_send()
    others_rows = asked_vmem.at[pl.ds(0, away)]
    drain(others_rows, others_rows, 1).wait_send()
    geos.wait_send()
    for arrived in gots:
        arrived.wait_send()


def sum_kernel(chunks, wanted_ref, back_ref, out_ref, arrived, first, second, in_sems, out_sems):
    ends = back_ref.shape[1]
    count = ends // chunks

    def piece(half, chunk):
        part = pl.ds(chunk * count, count)
        return pltpu.make_async_copy(
            back_ref.at[half, part], arrived.at[half, part], in_sems.at[half * chunks + chunk]
        )

    for chunk in range(chunks):
        for half in range(2):
            piece(half, chunk).start()
    first[...] = jnp.zeros_like(first)
    second[...] = jnp.zeros_like(second)
    for chunk in range(chunks):
        for half in range(2):
            piece(half, chunk).wait()

        @pl.loop(0, count, unroll=8)
        def _(index):
            slot = chunk * count + index
            place = pl.ds(pl.multiple_of(wanted_ref[slot] * P_SIZE, P_SIZE), P_SIZE)
            one = arrived[0, slot].astype(jnp.float32)
            two = arrived[1, slot].astype(jnp.float32)
            one_total, two_total = first[:, place], second[:, place]
            first[:, place] = one_total + one
            second[:, place] = two_total + two

    written = []
    for half, total in enumerate((first, second)):
        rows = pl.ds(half * HALF, HALF)
        written.append(pltpu.make_async_copy(total, out_ref.at[rows], out_sems.at[half]))
        written[-1].start()
    for copy in written:
        copy.wait()


def local(modes, geometry, pair_list, pair_kind):
    groups = lax.axis_size("grp")
    members = lax.axis_size("dev")
    devices = groups * members
    side = math.isqrt(members)
    local_count = modes.shape[1] // P_SIZE
    slots = pair_list.shape[0]
    ends = 2 * slots

    anywhere = pl.BlockSpec(memory_space=pl.ANY)
    smem = pl.BlockSpec(memory_space=pltpu.SMEM)
    back, wanted = pl.pallas_call(
        functools.partial(exchange_kernel, groups, members, side),
        out_shape=[
            jax.ShapeDtypeStruct((2, ends, HALF, P_SIZE), jnp.bfloat16),
            jax.ShapeDtypeStruct((ends,), jnp.int32),
        ],
        in_specs=[anywhere, anywhere, anywhere, anywhere],
        out_specs=[pl.BlockSpec(memory_space=pl.ANY), smem],
        scratch_shapes=[
            pltpu.VMEM((2, slots), jnp.int32),
            pltpu.VMEM((1, slots), jnp.int32),
            pltpu.VMEM(modes.shape, modes.dtype),
            pltpu.VMEM(geometry.shape, geometry.dtype),
            pltpu.VMEM((1, ends), jnp.int32),
            pltpu.SMEM((1, ends), jnp.int32),
            pltpu.VMEM((1, 128), jnp.int32),
            pltpu.VMEM((devices, 1, 128), jnp.int32),
            pltpu.SMEM((devices, 1, 128), jnp.int32),
            pltpu.VMEM((2, local_count, HALF, P_SIZE), jnp.bfloat16),
            pltpu.VMEM((local_count, 4, P_SIZE), jnp.float32),
            pltpu.VMEM((devices, 16, 128), jnp.int16),
            pltpu.VMEM((devices, 16, 128), jnp.int16),
            pltpu.VMEM((2, ends, HALF, P_SIZE), jnp.bfloat16),
            pltpu.VMEM((ends, HALF, P_SIZE), jnp.bfloat16),
            pltpu.VMEM((ends, HALF, P_SIZE), jnp.bfloat16),
            pltpu.VMEM((2, ends, HALF, P_SIZE), jnp.bfloat16),
            pltpu.VMEM((ends, P_SIZE, P_SIZE), jnp.bfloat16),
            pltpu.SemaphoreType.DMA((7,)),
            pltpu.SemaphoreType.DMA((7,)),
            pltpu.SemaphoreType.DMA((8,)),
            pltpu.SemaphoreType.DMA((8,)),
            pltpu.SemaphoreType.DMA,
            pltpu.SemaphoreType.DMA((4,)),
        ],
        compiler_params=pltpu.CompilerParams(
            collective_id=0, has_side_effects=True, vmem_limit_bytes=56 * 1024 * 1024
        ),
    )(pair_list.T, pair_kind.reshape(1, slots), modes, geometry)

    chunks = min(8, ends // 8)
    return pl.pallas_call(
        functools.partial(sum_kernel, chunks),
        out_shape=jax.ShapeDtypeStruct((2 * HALF, local_count * P_SIZE), jnp.float32),
        in_specs=[smem, anywhere],
        out_specs=anywhere,
        scratch_shapes=[
            pltpu.VMEM((2, ends, HALF, P_SIZE), jnp.bfloat16),
            pltpu.VMEM((HALF, local_count * P_SIZE), jnp.float32),
            pltpu.VMEM((HALF, local_count * P_SIZE), jnp.float32),
            pltpu.SemaphoreType.DMA((2 * chunks,)),
            pltpu.SemaphoreType.DMA((2,)),
        ],
        compiler_params=pltpu.CompilerParams(vmem_limit_bytes=56 * 1024 * 1024),
    )(wanted, back)


def solution(mesh):
    placed = (
        P(None, ("grp", "dev")),
        P(None, ("grp", "dev")),
        P(("grp", "dev"), None),
        P(("grp", "dev")),
    )
    return jax.shard_map(
        local, mesh=mesh, in_specs=placed, out_specs=P(None, ("grp", "dev")), check_vma=False
    )
```

```python
import functools
import math

import jax
import jax.numpy as jnp
from jax import lax
from jax.experimental import pallas as pl
from jax.experimental.pallas import tpu as pltpu
from jax.sharding import PartitionSpec as P

P_SIZE = 256
HALF = 16
X_STEPS = 32767.0 / 2.4
A_STEPS = 32767.0 / 2.0
FOUR_PI = 4.0 * math.pi
MESH = pl.DeviceIdType.MESH


def thirds(value):
    high = value.astype(jnp.bfloat16).astype(jnp.float32)
    rest = value - high
    mid = rest.astype(jnp.bfloat16).astype(jnp.float32)
    return high, mid, rest - mid


def column(row):
    count = row.shape[1]
    down = lax.broadcasted_iota(jnp.int32, (count, count), 0)
    across = lax.broadcasted_iota(jnp.int32, (count, count), 1)
    return jnp.sum(jnp.where(down == across, row, 0), axis=1, keepdims=True)


def slot_table(pair_ids, kinds, local_count):
    slots = pair_ids.shape[1]
    ends = 2 * slots
    left, right = pair_ids[0:1], pair_ids[1:2]
    ids = jnp.concatenate([left, right], axis=1)
    holder = lax.div(ids, local_count)
    down = lax.broadcasted_iota(jnp.int32, (ends, ends), 0)
    across = lax.broadcasted_iota(jnp.int32, (ends, ends), 1)
    holder_down = column(holder)
    same = holder_down == holder
    rank = jnp.sum(jnp.where(same & (down < across), 1, 0), axis=0, keepdims=True)
    rank_down = jnp.sum(jnp.where(same & (across < down), 1, 0), axis=1, keepdims=True)
    place = 2 * holder + rank
    other = jnp.concatenate([place[:, slots:], place[:, :slots]], axis=1)
    live = jnp.where(kinds > 0, 1, 0)
    twice = jnp.where(left != right, live, 0)
    keep = jnp.concatenate([live, twice], axis=1)
    admissible = jnp.where(kinds == 2, 1, 0)
    admissible = jnp.concatenate([admissible, admissible], axis=1)
    code = lax.rem(ids, local_count) + 64 * other + 16384 * admissible + 32768 * keep
    code_down = column(code)
    place_down = 2 * holder_down + rank_down
    table = jnp.sum(jnp.where(place_down == across, code_down, 0), axis=0, keepdims=True)
    asked = (code_down & 63) * (1 + 63 * rank_down)
    lanes = lax.broadcasted_iota(jnp.int32, (ends, 128), 1)
    request = jnp.sum(jnp.where(holder_down == lanes, asked, 0), axis=0, keepdims=True)
    return table, request


def sum_table(ids, local_count):
    ends = ids.shape[1]
    down = lax.broadcasted_iota(jnp.int32, (ends, ends), 0)
    across = lax.broadcasted_iota(jnp.int32, (ends, ends), 1)
    ids_down = column(ids)
    earlier = jnp.where((ids == ids_down) & (across < down), 1, 0)
    earlier = jnp.sum(earlier, axis=1, keepdims=True)
    place = earlier + jnp.sum(jnp.where(ids < ids_down, 1, 0), axis=1, keepdims=True)
    slot = lax.broadcasted_iota(jnp.int32, (ends, 1), 0) + 256 * jnp.minimum(earlier, 1)
    order = jnp.sum(jnp.where(place == across, slot, 0), axis=0, keepdims=True)
    lanes = lax.broadcasted_iota(jnp.int32, (ends, 128), 1)
    upto = jnp.sum(jnp.where(ids_down <= lanes, 1, 0), axis=0, keepdims=True)
    here = jnp.sum(jnp.where(ids_down == lanes, 1, 0), axis=0, keepdims=True)
    last = jnp.maximum(upto - 1, 0) + 256 * jnp.minimum(here, 1)
    return order, last


def exchange_kernel(
    groups, members, side,
    pair_hbm, kind_hbm, modes_hbm, geo_hbm,
    back_ref, total_ref, wanted_ref,
    pair_ref, kind_ref, modes_ref, geo_ref,
    code_vmem, code_smem, row_vmem, asked_vmem, asked_smem,
    mode_blocks, geo_blocks, geo_stage, geo_got,
    mode_stage, first_got, second_got, mode_back, tiles,
    wanted_smem, wanted_vmem, order_vmem, order_smem, last_vmem, last_smem,
    first_back, staged, first_total,
    send_sems, recv_sems, column_sems, row_sems, local_sem, input_sems,
):
    devices = groups * members
    others = devices - 1
    local_count = geo_blocks.shape[0]
    grp = lax.axis_index("grp")
    dev = lax.axis_index("dev")
    me = grp * members + dev
    member_bits = members.bit_length() - 1
    side_bits = side.bit_length() - 1

    def partner_of(step):
        shift = (step * 107) & (devices - 1)
        dg, dv = shift >> member_bits, shift & (members - 1)
        y = ((grp >> 1) + (dg >> 1)) & (groups // 2 - 1)
        core = (grp + dg) & 1
        x = ((dev >> side_bits) + (dv >> side_bits)) & (side - 1)
        z = (dev + dv) & (side - 1)
        return y * 2 + core, x * side + z

    my_y, my_core, my_x, my_z = grp >> 1, grp & 1, dev >> side_bits, dev & (side - 1)

    def at(dy, core, dx, dz):
        y = (my_y + dy) & (groups // 2 - 1)
        x, z = (my_x + dx) & (side - 1), (my_z + dz) & (side - 1)
        return y * 2 + ((my_core + core) & 1), x * side + z

    def in_column(which, index):
        return at(index >> 1, index & 1, which >> side_bits, which & (side - 1))

    my_key = dev * groups + grp
    my_rows = pl.ds(dev * groups, groups)

    def at_step(step, body):
        place = partner_of(step)
        body(step, place, place[0] * members + place[1])

    def two_steps(passes, body):
        @pl.loop(0, passes)
        def _(index):
            for step in (2 * index + 1, 2 * index + 2):
                at_step(step, body)

    def send(source, target, which, place):
        pltpu.make_async_remote_copy(
            src_ref=source, dst_ref=target,
            send_sem=send_sems.at[which], recv_sem=recv_sems.at[which],
            device_id=place, device_id_type=MESH,
        ).start()

    def drain(source, target, which):
        return pltpu.make_async_remote_copy(
            src_ref=source, dst_ref=target,
            send_sem=send_sems.at[which], recv_sem=recv_sems.at[which],
            device_id=(grp, dev), device_id_type=MESH,
        )

    barrier = pltpu.get_barrier_semaphore()
    for which in range(1, members):
        pl.semaphore_signal(barrier, inc=1, device_id=in_column(which, 0), device_id_type=MESH)
    for index in range(1, groups):
        pl.semaphore_signal(barrier, inc=1, device_id=in_column(0, index), device_id_type=MESH)

    inputs = [
        pltpu.make_async_copy(source, target, input_sems.at[index])
        for index, (source, target) in enumerate((
            (pair_hbm, pair_ref), (kind_hbm, kind_ref), (geo_hbm, geo_ref), (modes_hbm, modes_ref),
        ))
    ]
    for copy in inputs:
        copy.start()
    inputs[0].wait()
    inputs[1].wait()
    table, request = slot_table(pair_ref[...], kind_ref[...], local_count)
    row_vmem[...] = request
    asked_vmem[my_key] = request
    code_vmem[...] = table
    local = pltpu.make_async_copy(code_vmem, code_smem, local_sem)
    local.start()
    high_rows = lax.broadcasted_iota(jnp.int32, (4, P_SIZE), 0)
    steps = jnp.where(high_rows < 3, X_STEPS, A_STEPS)
    inputs[2].wait()
    inputs[3].wait()
    for cluster in range(local_count):
        panels = slice(cluster * P_SIZE, (cluster + 1) * P_SIZE)
        mode_blocks[0, cluster] = modes_ref[0:HALF, panels]
        mode_blocks[1, cluster] = modes_ref[HALF : 2 * HALF, panels]
        geo_blocks[cluster] = jnp.round(geo_ref[:, panels] * steps)
    local.wait()
    pl.semaphore_wait(barrier, members + groups - 2)

    for index in range(1, groups):
        send(row_vmem, asked_vmem.at[my_key], 0, in_column(0, index))
    in_own = drain(asked_vmem.at[pl.ds(0, groups - 1)], asked_vmem.at[pl.ds(0, groups - 1)], 0)
    in_own.wait_recv()

    def across(which, mark):
        return pltpu.make_async_remote_copy(
            src_ref=asked_vmem.at[my_rows], dst_ref=asked_vmem.at[my_rows],
            send_sem=send_sems.at[1], recv_sem=column_sems.at[mark],
            device_id=in_column(which, 0), device_id_type=MESH,
        )

    def readable(which):
        rows = pl.ds(in_column(which, 0)[1] * groups, groups)
        return pltpu.make_async_copy(asked_vmem.at[rows], asked_smem.at[rows], row_sems.at[which])

    for which in range(1, members):
        back_x, back_z = -(which // side) % side, -which % side
        across(which, back_x * side + back_z).start()
    local = readable(0)
    local.start()
    local.wait()

    def wanted(to, rank):
        key = (to & (members - 1)) * groups + (to >> member_bits)
        return (asked_smem[key, 0, me] >> (6 * rank)) & 63

    def geo_for(to):
        both = jnp.concatenate([geo_blocks[wanted(to, 0)], geo_blocks[wanted(to, 1)]], axis=0)
        both = jnp.concatenate([both[:, :128], both[:, 128:]], axis=0)
        return both.astype(jnp.int32).astype(jnp.int16)

    def send_geo(step, place, to):
        geo_stage[to] = geo_for(to)
        send(geo_stage.at[to], geo_got.at[me], 2, place)

    def send_modes(half, got):
        def body(step, place, to):
            for rank in range(2):
                mode_stage[half, 2 * to + rank] = mode_blocks[half, wanted(to, rank)]
            send(
                mode_stage.at[half, pl.ds(2 * to, 2)], got.at[pl.ds(2 * me, 2)], 3 + half, place
            )
        return body

    def at_place(place, body):
        body(0, place, place[0] * members + place[1])

    send_first = send_modes(0, first_got)
    send_second = send_modes(1, second_got)

    for body in (send_geo,):
        @pl.loop(1, groups)
        def _(index):
            at_place(in_column(0, index), body)

    def geos_for(which):
        readable(which).wait()

        @pl.loop(0, groups // 2)
        def _(index):
            at_place(in_column(which, 2 * index), send_geo)
            at_place(in_column(which, 2 * index + 1), send_geo)

    across(1, 1).wait_recv()
    readable(1).start()

    @pl.loop(1, members - 1)
    def _(which):
        across(which + 1, which + 1).wait_recv()
        readable(which + 1).start()
        geos_for(which)

    geos_for(members - 1)

    away = (members - 1) * groups
    for body in (send_first, send_second):
        @pl.loop(0, others // 2 + 1)
        def _(index):
            for step in (2 * index + 1, 2 * index + 2):
                @pl.when(step != devices)
                def _():
                    at_step(step, body)

    geo_got[me] = geo_for(me)
    for rank in range(2):
        first_got[2 * me + rank] = mode_blocks[0, wanted(me, rank)]
        second_got[2 * me + rank] = mode_blocks[1, wanted(me, rank)]

    @pl.loop(0, devices)
    def _(to):
        for rank in range(2):
            cluster = wanted(to, rank)
            wanted_smem[0, 2 * to + rank] = cluster

    def move(source, target):
        copy = pltpu.make_async_copy(source, target, local_sem)
        copy.start()
        copy.wait()

    geos = drain(geo_stage.at[pl.ds(0, others)], geo_got.at[pl.ds(0, others)], 2)
    geos.wait_recv()

    row = lax.broadcasted_iota(jnp.int32, (8, P_SIZE), 0)
    scale = jnp.where(
        (row & 3) < 3, FOUR_PI / X_STEPS, FOUR_PI * FOUR_PI / A_STEPS
    )

    def both_clusters(source):
        block = geo_got[source].astype(jnp.int32).astype(jnp.float32)
        return jnp.concatenate([block[0:8], block[8:16]], axis=1) * scale

    def length(block, factor):
        square = block * block
        return square[0:1] + square[1:2] + square[2:3] + block[3:4] * factor

    def tile_of(to, rank):
        code = code_smem[0, 2 * to + rank]
        other = (code >> 6) & 255
        factor = jnp.where((code & 16384) != 0, jnp.float32(0.1), jnp.float32(1.0))
        mine = both_clusters(to)
        theirs = both_clusters(other >> 1)
        if rank == 1:
            mine = pltpu.roll(mine, 4, 0)
        theirs = jnp.where((other & 1) == 1, pltpu.roll(theirs, 4, 0), theirs)
        norm = length(mine, factor)
        right = jnp.where(row < 3, mine, jnp.where(row == 3, norm, jnp.where(row == 4, 1.0, 0.0)))
        norm = length(theirs, factor)
        left = jnp.where(
            row < 3, -2.0 * theirs, jnp.where(row == 3, 1.0, jnp.where(row == 4, norm, 0.0))
        )
        a, b, c = thirds(left)
        left = jnp.concatenate([a, b, a, b, c, a], axis=0).astype(jnp.bfloat16)
        a, b, c = thirds(right)
        right = jnp.concatenate([a, a, b, b, a, c], axis=0).astype(jnp.bfloat16)
        squared = lax.dot_general(
            left, right, (((0,), (0,)), ((), ())), preferred_element_type=jnp.float32
        )
        return lax.rsqrt(squared).astype(jnp.bfloat16)

    def make_tiles(step, place, to):
        for rank in range(2):
            tiles[2 * (step - 1) + rank] = tile_of(to, rank)

    two_steps(devices // 2, make_tiles)

    def product(half, got, step, to, rank):
        code = code_smem[0, 2 * to + rank]
        keep = ((code >> 15) & 1).astype(jnp.float32)
        out = jnp.dot(
            got[(code >> 6) & 255], tiles[2 * (step - 1) + rank], preferred_element_type=jnp.float32
        )
        mode_back[half, 2 * to + rank] = (out * keep).astype(jnp.bfloat16)

    backs = (first_back, back_ref)

    def return_half(half, got):
        def give_back(to, place):
            send(
                mode_back.at[half, pl.ds(2 * to, 2)], backs[half].at[pl.ds(2 * me, 2)],
                5 + half, place,
            )

        def two_products(first, second):
            places = []
            for step in (first, second):
                place = partner_of(step)
                to = place[0] * members + place[1]
                places.append((to, place))
                for rank in range(2):
                    product(half, got, step, to, rank)
            return places

        @pl.loop(0, devices // 2 - 1)
        def _(index):
            for to, place in two_products(2 * index + 1, 2 * index + 2):
                give_back(to, place)

        give_back(*two_products(others, devices)[0])

    gots = []
    for half, got in enumerate((first_got, second_got)):
        arrived = drain(
            mode_stage.at[half, pl.ds(0, 2 * others)], got.at[pl.ds(0, 2 * others)], 3 + half
        )
        arrived.wait_recv()
        gots.append(arrived)
        return_half(half, got)

    for rank in range(2):
        first_back[2 * me + rank] = mode_back[0, 2 * me + rank]
    move(mode_back.at[1, pl.ds(2 * me, 2)], back_ref.at[pl.ds(2 * me, 2)])

    move(wanted_smem, wanted_vmem)
    move(wanted_vmem, wanted_ref)
    order_vmem[...], last_vmem[...] = sum_table(wanted_vmem[...], local_count)
    move(order_vmem, order_smem)
    move(last_vmem, last_smem)
    returned = [
        drain(mode_back.at[half, pl.ds(0, 2 * others)], backs[half].at[pl.ds(0, 2 * others)], 5 + half)
        for half in range(2)
    ]
    returned[0].wait_recv()

    def add(index, total):
        code = order_smem[0, index]
        total = total * (code >> 8).astype(jnp.float32) + first_back[code & 255].astype(jnp.float32)
        staged[index] = total
        return total

    lax.fori_loop(0, 2 * devices, add, jnp.zeros((HALF, P_SIZE), jnp.float32), unroll=4)
    for cluster in range(local_count):
        code = last_smem[0, cluster]
        first_total[:, cluster * P_SIZE : (cluster + 1) * P_SIZE] = (
            staged[code & 255] * (code >> 8).astype(jnp.float32)
        )
    move(first_total, total_ref)
    returned[1].wait_recv()
    for copy in returned:
        copy.wait_send()
    in_own.wait_send()
    others_rows = asked_vmem.at[pl.ds(0, away)]
    drain(others_rows, others_rows, 1).wait_send()
    geos.wait_send()
    for arrived in gots:
        arrived.wait_send()


def sum_kernel(
    chunks, wanted_hbm, back_ref, total_ref, out_ref, wanted_ref, arrived, first, second, in_sems, out_sems
):
    ends = back_ref.shape[0]
    count = ends // chunks

    def piece(chunk):
        part = pl.ds(chunk * count, count)
        return pltpu.make_async_copy(back_ref.at[part], arrived.at[part], in_sems.at[chunk])

    known = pltpu.make_async_copy(wanted_hbm, wanted_ref, in_sems.at[chunks + 1])
    known.start()
    for chunk in range(chunks):
        piece(chunk).start()
    ready = pltpu.make_async_copy(total_ref, first, in_sems.at[chunks])
    ready.start()
    written = [
        pltpu.make_async_copy(first, out_ref.at[pl.ds(0, HALF)], out_sems.at[0]),
        pltpu.make_async_copy(second, out_ref.at[pl.ds(HALF, HALF)], out_sems.at[1]),
    ]
    second[...] = jnp.zeros_like(second)
    known.wait()
    for chunk in range(chunks):
        piece(chunk).wait()

        @pl.loop(0, count, unroll=8)
        def _(index):
            slot = chunk * count + index
            place = pl.ds(pl.multiple_of(wanted_ref[0, slot] * P_SIZE, P_SIZE), P_SIZE)
            second[:, place] += arrived[slot].astype(jnp.float32)

        if chunk == 1:
            ready.wait()
            written[0].start()

    written[1].start()
    for copy in written:
        copy.wait()


def local(modes, geometry, pair_list, pair_kind):
    groups = lax.axis_size("grp")
    members = lax.axis_size("dev")
    devices = groups * members
    side = math.isqrt(members)
    local_count = modes.shape[1] // P_SIZE
    slots = pair_list.shape[0]
    ends = 2 * slots

    anywhere = pl.BlockSpec(memory_space=pl.ANY)
    back, total, wanted = pl.pallas_call(
        functools.partial(exchange_kernel, groups, members, side),
        out_shape=[
            jax.ShapeDtypeStruct((ends, HALF, P_SIZE), jnp.bfloat16),
            jax.ShapeDtypeStruct((HALF, local_count * P_SIZE), jnp.float32),
            jax.ShapeDtypeStruct((1, ends), jnp.int32),
        ],
        in_specs=[anywhere, anywhere, anywhere, anywhere],
        out_specs=[anywhere, anywhere, anywhere],
        scratch_shapes=[
            pltpu.VMEM((2, slots), jnp.int32),
            pltpu.VMEM((1, slots), jnp.int32),
            pltpu.VMEM(modes.shape, modes.dtype),
            pltpu.VMEM(geometry.shape, geometry.dtype),
            pltpu.VMEM((1, ends), jnp.int32),
            pltpu.SMEM((1, ends), jnp.int32),
            pltpu.VMEM((1, 128), jnp.int32),
            pltpu.VMEM((devices, 1, 128), jnp.int32),
            pltpu.SMEM((devices, 1, 128), jnp.int32),
            pltpu.VMEM((2, local_count, HALF, P_SIZE), jnp.bfloat16),
            pltpu.VMEM((local_count, 4, P_SIZE), jnp.float32),
            pltpu.VMEM((devices, 16, 128), jnp.int16),
            pltpu.VMEM((devices, 16, 128), jnp.int16),
            pltpu.VMEM((2, ends, HALF, P_SIZE), jnp.bfloat16),
            pltpu.VMEM((ends, HALF, P_SIZE), jnp.bfloat16),
            pltpu.VMEM((ends, HALF, P_SIZE), jnp.bfloat16),
            pltpu.VMEM((2, ends, HALF, P_SIZE), jnp.bfloat16),
            pltpu.VMEM((ends, P_SIZE, P_SIZE), jnp.bfloat16),
            pltpu.SMEM((1, ends), jnp.int32),
            pltpu.VMEM((1, ends), jnp.int32),
            pltpu.VMEM((1, ends), jnp.int32),
            pltpu.SMEM((1, ends), jnp.int32),
            pltpu.VMEM((1, 128), jnp.int32),
            pltpu.SMEM((1, 128), jnp.int32),
            pltpu.VMEM((ends, HALF, P_SIZE), jnp.bfloat16),
            pltpu.VMEM((ends, HALF, P_SIZE), jnp.float32),
            pltpu.VMEM((HALF, local_count * P_SIZE), jnp.float32),
            pltpu.SemaphoreType.DMA((7,)),
            pltpu.SemaphoreType.DMA((7,)),
            pltpu.SemaphoreType.DMA((members,)),
            pltpu.SemaphoreType.DMA((members,)),
            pltpu.SemaphoreType.DMA,
            pltpu.SemaphoreType.DMA((4,)),
        ],
        compiler_params=pltpu.CompilerParams(
            collective_id=0, has_side_effects=True, vmem_limit_bytes=58 * 1024 * 1024
        ),
    )(pair_list.T, pair_kind.reshape(1, slots), modes, geometry)

    chunks = 4
    return pl.pallas_call(
        functools.partial(sum_kernel, chunks),
        out_shape=jax.ShapeDtypeStruct((2 * HALF, local_count * P_SIZE), jnp.float32),
        in_specs=[anywhere, anywhere, anywhere],
        out_specs=anywhere,
        scratch_shapes=[
            pltpu.SMEM((1, ends), jnp.int32),
            pltpu.VMEM((ends, HALF, P_SIZE), jnp.bfloat16),
            pltpu.VMEM((HALF, local_count * P_SIZE), jnp.float32),
            pltpu.VMEM((HALF, local_count * P_SIZE), jnp.float32),
            pltpu.SemaphoreType.DMA((chunks + 2,)),
            pltpu.SemaphoreType.DMA((2,)),
        ],
        compiler_params=pltpu.CompilerParams(vmem_limit_bytes=58 * 1024 * 1024),
    )(wanted, back, total)


def solution(mesh):
    placed = (
        P(None, ("grp", "dev")),
        P(None, ("grp", "dev")),
        P(("grp", "dev"), None),
        P(("grp", "dev")),
    )
    return jax.shard_map(
        local, mesh=mesh, in_specs=placed, out_specs=P(None, ("grp", "dev")), check_vma=False
    )
```

```python
import functools
import math

import jax
import jax.numpy as jnp
from jax import lax
from jax.experimental import pallas as pl
from jax.experimental.pallas import tpu as pltpu
from jax.sharding import PartitionSpec as P

P_SIZE = 256
HALF = 16
X_STEPS = 32767.0 / 2.4
A_STEPS = 32767.0 / 2.0
FOUR_PI = 4.0 * math.pi
MESH = pl.DeviceIdType.MESH


def thirds(value):
    high = value.astype(jnp.bfloat16).astype(jnp.float32)
    rest = value - high
    mid = rest.astype(jnp.bfloat16).astype(jnp.float32)
    return high, mid, rest - mid


def column(row):
    count = row.shape[1]
    down = lax.broadcasted_iota(jnp.int32, (count, count), 0)
    across = lax.broadcasted_iota(jnp.int32, (count, count), 1)
    return jnp.sum(jnp.where(down == across, row, 0), axis=1, keepdims=True)


def slot_table(pair_ids, kinds, local_count):
    slots = pair_ids.shape[1]
    ends = 2 * slots
    left, right = pair_ids[0:1], pair_ids[1:2]
    ids = jnp.concatenate([left, right], axis=1)
    holder = lax.div(ids, local_count)
    down = lax.broadcasted_iota(jnp.int32, (ends, ends), 0)
    across = lax.broadcasted_iota(jnp.int32, (ends, ends), 1)
    holder_down = column(holder)
    same = holder_down == holder
    rank = jnp.sum(jnp.where(same & (down < across), 1, 0), axis=0, keepdims=True)
    rank_down = jnp.sum(jnp.where(same & (across < down), 1, 0), axis=1, keepdims=True)
    place = 2 * holder + rank
    other = jnp.concatenate([place[:, slots:], place[:, :slots]], axis=1)
    live = jnp.where(kinds > 0, 1, 0)
    twice = jnp.where(left != right, live, 0)
    keep = jnp.concatenate([live, twice], axis=1)
    admissible = jnp.where(kinds == 2, 1, 0)
    admissible = jnp.concatenate([admissible, admissible], axis=1)
    code = lax.rem(ids, local_count) + 64 * other + 16384 * admissible + 32768 * keep
    code_down = column(code)
    place_down = 2 * holder_down + rank_down
    table = jnp.sum(jnp.where(place_down == across, code_down, 0), axis=0, keepdims=True)
    asked = (code_down & 63) * (1 + 63 * rank_down)
    lanes = lax.broadcasted_iota(jnp.int32, (ends, 128), 1)
    request = jnp.sum(jnp.where(holder_down == lanes, asked, 0), axis=0, keepdims=True)
    return table, request


def sum_table(ids, local_count):
    ends = ids.shape[1]
    down = lax.broadcasted_iota(jnp.int32, (ends, ends), 0)
    across = lax.broadcasted_iota(jnp.int32, (ends, ends), 1)
    ids_down = column(ids)
    earlier = jnp.where((ids == ids_down) & (across < down), 1, 0)
    earlier = jnp.sum(earlier, axis=1, keepdims=True)
    place = earlier + jnp.sum(jnp.where(ids < ids_down, 1, 0), axis=1, keepdims=True)
    slot = lax.broadcasted_iota(jnp.int32, (ends, 1), 0) + 256 * jnp.minimum(earlier, 1)
    order = jnp.sum(jnp.where(place == across, slot, 0), axis=0, keepdims=True)
    lanes = lax.broadcasted_iota(jnp.int32, (ends, 128), 1)
    upto = jnp.sum(jnp.where(ids_down <= lanes, 1, 0), axis=0, keepdims=True)
    here = jnp.sum(jnp.where(ids_down == lanes, 1, 0), axis=0, keepdims=True)
    last = jnp.maximum(upto - 1, 0) + 256 * jnp.minimum(here, 1)
    return order, last


def exchange_kernel(
    groups, members, side,
    pair_hbm, kind_hbm, modes_hbm, geo_hbm,
    back_ref, total_ref, wanted_ref,
    pair_ref, kind_ref, modes_ref, geo_ref,
    code_vmem, code_smem, row_vmem, asked_vmem, asked_smem,
    mode_blocks, geo_blocks, geo_stage, geo_got,
    mode_stage, first_got, second_got, mode_back, tiles,
    wanted_smem, wanted_vmem, order_vmem, order_smem, last_vmem, last_smem,
    first_back, staged, first_total,
    send_sems, recv_sems, column_sems, row_sems, local_sem, input_sems,
):
    devices = groups * members
    others = devices - 1
    local_count = geo_blocks.shape[0]
    grp = lax.axis_index("grp")
    dev = lax.axis_index("dev")
    me = grp * members + dev
    member_bits = members.bit_length() - 1
    side_bits = side.bit_length() - 1

    def partner_of(step):
        shift = (step * 53) & (devices - 1)
        dg, dv = shift >> member_bits, shift & (members - 1)
        y = ((grp >> 1) + (dg >> 1)) & (groups // 2 - 1)
        core = (grp + dg) & 1
        x = ((dev >> side_bits) + (dv >> side_bits)) & (side - 1)
        z = (dev + dv) & (side - 1)
        return y * 2 + core, x * side + z

    my_y, my_core, my_x, my_z = grp >> 1, grp & 1, dev >> side_bits, dev & (side - 1)

    def at(dy, core, dx, dz):
        y = (my_y + dy) & (groups // 2 - 1)
        x, z = (my_x + dx) & (side - 1), (my_z + dz) & (side - 1)
        return y * 2 + ((my_core + core) & 1), x * side + z

    def in_column(which, index):
        return at(index >> 1, index & 1, which >> side_bits, which & (side - 1))

    my_key = dev * groups + grp
    my_rows = pl.ds(dev * groups, groups)

    def at_step(step, body):
        place = partner_of(step)
        body(step, place, place[0] * members + place[1])

    def two_steps(passes, body):
        @pl.loop(0, passes)
        def _(index):
            for step in (2 * index + 1, 2 * index + 2):
                at_step(step, body)

    def send(source, target, which, place):
        pltpu.make_async_remote_copy(
            src_ref=source, dst_ref=target,
            send_sem=send_sems.at[which], recv_sem=recv_sems.at[which],
            device_id=place, device_id_type=MESH,
        ).start()

    def drain(source, target, which):
        return pltpu.make_async_remote_copy(
            src_ref=source, dst_ref=target,
            send_sem=send_sems.at[which], recv_sem=recv_sems.at[which],
            device_id=(grp, dev), device_id_type=MESH,
        )

    barrier = pltpu.get_barrier_semaphore()
    for which in range(1, members):
        pl.semaphore_signal(barrier, inc=1, device_id=in_column(which, 0), device_id_type=MESH)
    for index in range(1, groups):
        pl.semaphore_signal(barrier, inc=1, device_id=in_column(0, index), device_id_type=MESH)

    inputs = [
        pltpu.make_async_copy(source, target, input_sems.at[index])
        for index, (source, target) in enumerate((
            (pair_hbm, pair_ref), (kind_hbm, kind_ref), (geo_hbm, geo_ref), (modes_hbm, modes_ref),
        ))
    ]
    for copy in inputs:
        copy.start()
    inputs[0].wait()
    inputs[1].wait()
    table, request = slot_table(pair_ref[...], kind_ref[...], local_count)
    row_vmem[...] = request
    asked_vmem[my_key] = request
    code_vmem[...] = table
    local = pltpu.make_async_copy(code_vmem, code_smem, local_sem)
    local.start()
    high_rows = lax.broadcasted_iota(jnp.int32, (4, P_SIZE), 0)
    steps = jnp.where(high_rows < 3, X_STEPS, A_STEPS)
    inputs[2].wait()
    inputs[3].wait()
    for cluster in range(local_count):
        panels = slice(cluster * P_SIZE, (cluster + 1) * P_SIZE)
        mode_blocks[0, cluster] = modes_ref[0:HALF, panels]
        mode_blocks[1, cluster] = modes_ref[HALF : 2 * HALF, panels]
        geo_blocks[cluster] = jnp.round(geo_ref[:, panels] * steps)
    local.wait()
    pl.semaphore_wait(barrier, members + groups - 2)

    for index in range(1, groups):
        send(row_vmem, asked_vmem.at[my_key], 0, in_column(0, index))
    in_own = drain(asked_vmem.at[pl.ds(0, groups - 1)], asked_vmem.at[pl.ds(0, groups - 1)], 0)
    in_own.wait_recv()

    def across(which, mark):
        return pltpu.make_async_remote_copy(
            src_ref=asked_vmem.at[my_rows], dst_ref=asked_vmem.at[my_rows],
            send_sem=send_sems.at[1], recv_sem=column_sems.at[mark],
            device_id=in_column(which, 0), device_id_type=MESH,
        )

    def readable(which):
        rows = pl.ds(in_column(which, 0)[1] * groups, groups)
        return pltpu.make_async_copy(asked_vmem.at[rows], asked_smem.at[rows], row_sems.at[which])

    for which in range(1, members):
        back_x, back_z = -(which // side) % side, -which % side
        across(which, back_x * side + back_z).start()
    local = readable(0)
    local.start()
    local.wait()

    def wanted(to, rank):
        key = (to & (members - 1)) * groups + (to >> member_bits)
        return (asked_smem[key, 0, me] >> (6 * rank)) & 63

    def geo_for(to):
        both = jnp.concatenate([geo_blocks[wanted(to, 0)], geo_blocks[wanted(to, 1)]], axis=0)
        both = jnp.concatenate([both[:, :128], both[:, 128:]], axis=0)
        return both.astype(jnp.int32).astype(jnp.int16)

    def send_geo(step, place, to):
        geo_stage[to] = geo_for(to)
        send(geo_stage.at[to], geo_got.at[me], 2, place)

    def send_modes(half, got):
        def body(step, place, to):
            for rank in range(2):
                mode_stage[half, 2 * to + rank] = mode_blocks[half, wanted(to, rank)]
            send(
                mode_stage.at[half, pl.ds(2 * to, 2)], got.at[pl.ds(2 * me, 2)], 3 + half, place
            )
        return body

    def at_place(place, body):
        body(0, place, place[0] * members + place[1])

    send_first = send_modes(0, first_got)
    send_second = send_modes(1, second_got)

    for body in (send_geo,):
        @pl.loop(1, groups)
        def _(index):
            at_place(in_column(0, index), body)

    def geos_for(which):
        readable(which).wait()

        @pl.loop(0, groups // 2)
        def _(index):
            at_place(in_column(which, 2 * index), send_geo)
            at_place(in_column(which, 2 * index + 1), send_geo)

    across(1, 1).wait_recv()
    readable(1).start()

    @pl.loop(1, members - 1)
    def _(which):
        across(which + 1, which + 1).wait_recv()
        readable(which + 1).start()
        geos_for(which)

    geos_for(members - 1)

    away = (members - 1) * groups
    for body in (send_first, send_second):
        @pl.loop(0, others // 2 + 1)
        def _(index):
            for step in (2 * index + 1, 2 * index + 2):
                @pl.when(step != devices)
                def _():
                    at_step(step, body)

    geo_got[me] = geo_for(me)
    for rank in range(2):
        first_got[2 * me + rank] = mode_blocks[0, wanted(me, rank)]
        second_got[2 * me + rank] = mode_blocks[1, wanted(me, rank)]

    @pl.loop(0, devices)
    def _(to):
        for rank in range(2):
            cluster = wanted(to, rank)
            wanted_smem[0, 2 * to + rank] = cluster

    def move(source, target):
        copy = pltpu.make_async_copy(source, target, local_sem)
        copy.start()
        copy.wait()

    geos = drain(geo_stage.at[pl.ds(0, others)], geo_got.at[pl.ds(0, others)], 2)
    geos.wait_recv()

    row = lax.broadcasted_iota(jnp.int32, (8, P_SIZE), 0)
    scale = jnp.where(
        (row & 3) < 3, FOUR_PI / X_STEPS, FOUR_PI * FOUR_PI / A_STEPS
    )

    def both_clusters(source):
        block = geo_got[source].astype(jnp.int32).astype(jnp.float32)
        return jnp.concatenate([block[0:8], block[8:16]], axis=1) * scale

    def length(block, factor):
        square = block * block
        return square[0:1] + square[1:2] + square[2:3] + block[3:4] * factor

    def tile_of(to, rank):
        code = code_smem[0, 2 * to + rank]
        other = (code >> 6) & 255
        factor = jnp.where((code & 16384) != 0, jnp.float32(0.1), jnp.float32(1.0))
        mine = both_clusters(to)
        theirs = both_clusters(other >> 1)
        if rank == 1:
            mine = pltpu.roll(mine, 4, 0)
        theirs = jnp.where((other & 1) == 1, pltpu.roll(theirs, 4, 0), theirs)
        norm = length(mine, factor)
        right = jnp.where(row < 3, mine, jnp.where(row == 3, norm, jnp.where(row == 4, 1.0, 0.0)))
        norm = length(theirs, factor)
        left = jnp.where(
            row < 3, -2.0 * theirs, jnp.where(row == 3, 1.0, jnp.where(row == 4, norm, 0.0))
        )
        a, b, c = thirds(left)
        left = jnp.concatenate([a, b, a, b, c, a], axis=0).astype(jnp.bfloat16)
        a, b, c = thirds(right)
        right = jnp.concatenate([a, a, b, b, a, c], axis=0).astype(jnp.bfloat16)
        squared = lax.dot_general(
            left, right, (((0,), (0,)), ((), ())), preferred_element_type=jnp.float32
        )
        return lax.rsqrt(squared).astype(jnp.bfloat16)

    def make_tiles(step, place, to):
        for rank in range(2):
            tiles[2 * (step - 1) + rank] = tile_of(to, rank)

    two_steps(devices // 2, make_tiles)

    def product(half, got, step, to, rank):
        code = code_smem[0, 2 * to + rank]
        keep = ((code >> 15) & 1).astype(jnp.float32)
        out = jnp.dot(
            got[(code >> 6) & 255], tiles[2 * (step - 1) + rank], preferred_element_type=jnp.float32
        )
        mode_back[half, 2 * to + rank] = (out * keep).astype(jnp.bfloat16)

    backs = (first_back, back_ref)

    def return_half(half, got):
        def give_back(to, place):
            send(
                mode_back.at[half, pl.ds(2 * to, 2)], backs[half].at[pl.ds(2 * me, 2)],
                5 + half, place,
            )

        def two_products(first, second):
            places = []
            for step in (first, second):
                place = partner_of(step)
                to = place[0] * members + place[1]
                places.append((to, place))
                for rank in range(2):
                    product(half, got, step, to, rank)
            return places

        @pl.loop(0, devices // 2 - 1)
        def _(index):
            for to, place in two_products(2 * index + 1, 2 * index + 2):
                give_back(to, place)

        give_back(*two_products(others, devices)[0])

    gots = []
    for half, got in enumerate((first_got, second_got)):
        arrived = drain(
            mode_stage.at[half, pl.ds(0, 2 * others)], got.at[pl.ds(0, 2 * others)], 3 + half
        )
        arrived.wait_recv()
        gots.append(arrived)
        return_half(half, got)

    for rank in range(2):
        first_back[2 * me + rank] = mode_back[0, 2 * me + rank]
    move(mode_back.at[1, pl.ds(2 * me, 2)], back_ref.at[pl.ds(2 * me, 2)])

    move(wanted_smem, wanted_vmem)
    move(wanted_vmem, wanted_ref)
    order_vmem[...], last_vmem[...] = sum_table(wanted_vmem[...], local_count)
    move(order_vmem, order_smem)
    move(last_vmem, last_smem)
    returned = [
        drain(mode_back.at[half, pl.ds(0, 2 * others)], backs[half].at[pl.ds(0, 2 * others)], 5 + half)
        for half in range(2)
    ]
    returned[0].wait_recv()

    def add(index, total):
        code = order_smem[0, index]
        total = total * (code >> 8).astype(jnp.float32) + first_back[code & 255].astype(jnp.float32)
        staged[index] = total
        return total

    lax.fori_loop(0, 2 * devices, add, jnp.zeros((HALF, P_SIZE), jnp.float32), unroll=4)
    for cluster in range(local_count):
        code = last_smem[0, cluster]
        first_total[:, cluster * P_SIZE : (cluster + 1) * P_SIZE] = (
            staged[code & 255] * (code >> 8).astype(jnp.float32)
        )
    move(first_total, total_ref)
    returned[1].wait_recv()
    for copy in returned:
        copy.wait_send()
    in_own.wait_send()
    others_rows = asked_vmem.at[pl.ds(0, away)]
    drain(others_rows, others_rows, 1).wait_send()
    geos.wait_send()
    for arrived in gots:
        arrived.wait_send()


def sum_kernel(
    chunks, wanted_hbm, back_ref, total_ref, out_ref, wanted_ref, arrived, first, second, in_sems, out_sems
):
    ends = back_ref.shape[0]
    count = ends // chunks

    def piece(chunk):
        part = pl.ds(chunk * count, count)
        return pltpu.make_async_copy(back_ref.at[part], arrived.at[part], in_sems.at[chunk])

    known = pltpu.make_async_copy(wanted_hbm, wanted_ref, in_sems.at[chunks + 1])
    known.start()
    for chunk in range(chunks):
        piece(chunk).start()
    ready = pltpu.make_async_copy(total_ref, first, in_sems.at[chunks])
    ready.start()
    written = [
        pltpu.make_async_copy(first, out_ref.at[pl.ds(0, HALF)], out_sems.at[0]),
        pltpu.make_async_copy(second, out_ref.at[pl.ds(HALF, HALF)], out_sems.at[1]),
    ]
    second[...] = jnp.zeros_like(second)
    known.wait()
    for chunk in range(chunks):
        piece(chunk).wait()

        @pl.loop(0, count, unroll=8)
        def _(index):
            slot = chunk * count + index
            place = pl.ds(pl.multiple_of(wanted_ref[0, slot] * P_SIZE, P_SIZE), P_SIZE)
            second[:, place] += arrived[slot].astype(jnp.float32)

        if chunk == 1:
            ready.wait()
            written[0].start()

    written[1].start()
    for copy in written:
        copy.wait()


def local(modes, geometry, pair_list, pair_kind):
    groups = lax.axis_size("grp")
    members = lax.axis_size("dev")
    devices = groups * members
    side = math.isqrt(members)
    local_count = modes.shape[1] // P_SIZE
    slots = pair_list.shape[0]
    ends = 2 * slots

    anywhere = pl.BlockSpec(memory_space=pl.ANY)
    back, total, wanted = pl.pallas_call(
        functools.partial(exchange_kernel, groups, members, side),
        out_shape=[
            jax.ShapeDtypeStruct((ends, HALF, P_SIZE), jnp.bfloat16),
            jax.ShapeDtypeStruct((HALF, local_count * P_SIZE), jnp.float32),
            jax.ShapeDtypeStruct((1, ends), jnp.int32),
        ],
        in_specs=[anywhere, anywhere, anywhere, anywhere],
        out_specs=[anywhere, anywhere, anywhere],
        scratch_shapes=[
            pltpu.VMEM((2, slots), jnp.int32),
            pltpu.VMEM((1, slots), jnp.int32),
            pltpu.VMEM(modes.shape, modes.dtype),
            pltpu.VMEM(geometry.shape, geometry.dtype),
            pltpu.VMEM((1, ends), jnp.int32),
            pltpu.SMEM((1, ends), jnp.int32),
            pltpu.VMEM((1, 128), jnp.int32),
            pltpu.VMEM((devices, 1, 128), jnp.int32),
            pltpu.SMEM((devices, 1, 128), jnp.int32),
            pltpu.VMEM((2, local_count, HALF, P_SIZE), jnp.bfloat16),
            pltpu.VMEM((local_count, 4, P_SIZE), jnp.float32),
            pltpu.VMEM((devices, 16, 128), jnp.int16),
            pltpu.VMEM((devices, 16, 128), jnp.int16),
            pltpu.VMEM((2, ends, HALF, P_SIZE), jnp.bfloat16),
            pltpu.VMEM((ends, HALF, P_SIZE), jnp.bfloat16),
            pltpu.VMEM((ends, HALF, P_SIZE), jnp.bfloat16),
            pltpu.VMEM((2, ends, HALF, P_SIZE), jnp.bfloat16),
            pltpu.VMEM((ends, P_SIZE, P_SIZE), jnp.bfloat16),
            pltpu.SMEM((1, ends), jnp.int32),
            pltpu.VMEM((1, ends), jnp.int32),
            pltpu.VMEM((1, ends), jnp.int32),
            pltpu.SMEM((1, ends), jnp.int32),
            pltpu.VMEM((1, 128), jnp.int32),
            pltpu.SMEM((1, 128), jnp.int32),
            pltpu.VMEM((ends, HALF, P_SIZE), jnp.bfloat16),
            pltpu.VMEM((ends, HALF, P_SIZE), jnp.float32),
            pltpu.VMEM((HALF, local_count * P_SIZE), jnp.float32),
            pltpu.SemaphoreType.DMA((7,)),
            pltpu.SemaphoreType.DMA((7,)),
            pltpu.SemaphoreType.DMA((members,)),
            pltpu.SemaphoreType.DMA((members,)),
            pltpu.SemaphoreType.DMA,
            pltpu.SemaphoreType.DMA((4,)),
        ],
        compiler_params=pltpu.CompilerParams(
            collective_id=0, has_side_effects=True, vmem_limit_bytes=58 * 1024 * 1024
        ),
    )(pair_list.T, pair_kind.reshape(1, slots), modes, geometry)

    chunks = 4
    return pl.pallas_call(
        functools.partial(sum_kernel, chunks),
        out_shape=jax.ShapeDtypeStruct((2 * HALF, local_count * P_SIZE), jnp.float32),
        in_specs=[anywhere, anywhere, anywhere],
        out_specs=anywhere,
        scratch_shapes=[
            pltpu.SMEM((1, ends), jnp.int32),
            pltpu.VMEM((ends, HALF, P_SIZE), jnp.bfloat16),
            pltpu.VMEM((HALF, local_count * P_SIZE), jnp.float32),
            pltpu.VMEM((HALF, local_count * P_SIZE), jnp.float32),
            pltpu.SemaphoreType.DMA((chunks + 2,)),
            pltpu.SemaphoreType.DMA((2,)),
        ],
        compiler_params=pltpu.CompilerParams(vmem_limit_bytes=58 * 1024 * 1024),
    )(wanted, back, total)


def solution(mesh):
    placed = (
        P(None, ("grp", "dev")),
        P(None, ("grp", "dev")),
        P(("grp", "dev"), None),
        P(("grp", "dev")),
    )
    return jax.shard_map(
        local, mesh=mesh, in_specs=placed, out_specs=P(None, ("grp", "dev")), check_vma=False
    )
```

```python
import functools
import math

import jax
import jax.numpy as jnp
from jax import lax
from jax.experimental import pallas as pl
from jax.experimental.pallas import tpu as pltpu
from jax.sharding import PartitionSpec as P

P_SIZE = 256
HALF = 16
X_STEPS = 32767.0 / 2.4
A_STEPS = 32767.0 / 2.0
FOUR_PI = 4.0 * math.pi
MESH = pl.DeviceIdType.MESH


def thirds(value):
    high = value.astype(jnp.bfloat16).astype(jnp.float32)
    rest = value - high
    mid = rest.astype(jnp.bfloat16).astype(jnp.float32)
    return high, mid, rest - mid


def column(row):
    count = row.shape[1]
    down = lax.broadcasted_iota(jnp.int32, (count, count), 0)
    across = lax.broadcasted_iota(jnp.int32, (count, count), 1)
    return jnp.sum(jnp.where(down == across, row, 0), axis=1, keepdims=True)


def slot_table(pair_ids, kinds, local_count):
    slots = pair_ids.shape[1]
    ends = 2 * slots
    left, right = pair_ids[0:1], pair_ids[1:2]
    ids = jnp.concatenate([left, right], axis=1)
    holder = lax.div(ids, local_count)
    down = lax.broadcasted_iota(jnp.int32, (ends, ends), 0)
    across = lax.broadcasted_iota(jnp.int32, (ends, ends), 1)
    holder_down = column(holder)
    same = holder_down == holder
    rank = jnp.sum(jnp.where(same & (down < across), 1, 0), axis=0, keepdims=True)
    rank_down = jnp.sum(jnp.where(same & (across < down), 1, 0), axis=1, keepdims=True)
    place = 2 * holder + rank
    other = jnp.concatenate([place[:, slots:], place[:, :slots]], axis=1)
    live = jnp.where(kinds > 0, 1, 0)
    twice = jnp.where(left != right, live, 0)
    keep = jnp.concatenate([live, twice], axis=1)
    admissible = jnp.where(kinds == 2, 1, 0)
    admissible = jnp.concatenate([admissible, admissible], axis=1)
    code = lax.rem(ids, local_count) + 64 * other + 16384 * admissible + 32768 * keep
    code_down = column(code)
    place_down = 2 * holder_down + rank_down
    table = jnp.sum(jnp.where(place_down == across, code_down, 0), axis=0, keepdims=True)
    asked = (code_down & 63) * (1 + 63 * rank_down)
    lanes = lax.broadcasted_iota(jnp.int32, (ends, 128), 1)
    request = jnp.sum(jnp.where(holder_down == lanes, asked, 0), axis=0, keepdims=True)
    return table, request


def sum_table(ids, local_count):
    ends = ids.shape[1]
    down = lax.broadcasted_iota(jnp.int32, (ends, ends), 0)
    across = lax.broadcasted_iota(jnp.int32, (ends, ends), 1)
    ids_down = column(ids)
    earlier = jnp.where((ids == ids_down) & (across < down), 1, 0)
    earlier = jnp.sum(earlier, axis=1, keepdims=True)
    place = earlier + jnp.sum(jnp.where(ids < ids_down, 1, 0), axis=1, keepdims=True)
    slot = lax.broadcasted_iota(jnp.int32, (ends, 1), 0) + 256 * jnp.minimum(earlier, 1)
    order = jnp.sum(jnp.where(place == across, slot, 0), axis=0, keepdims=True)
    lanes = lax.broadcasted_iota(jnp.int32, (ends, 128), 1)
    upto = jnp.sum(jnp.where(ids_down <= lanes, 1, 0), axis=0, keepdims=True)
    here = jnp.sum(jnp.where(ids_down == lanes, 1, 0), axis=0, keepdims=True)
    last = jnp.maximum(upto - 1, 0) + 256 * jnp.minimum(here, 1)
    return order, last


def exchange_kernel(
    groups, members, side,
    pair_hbm, kind_hbm, modes_hbm, geo_hbm,
    back_ref, total_ref, wanted_ref,
    pair_ref, kind_ref, modes_ref, geo_ref,
    code_vmem, code_smem, row_vmem, asked_vmem, asked_smem,
    mode_blocks, geo_blocks, geo_stage, geo_got,
    mode_stage, first_got, second_got, mode_back, tiles,
    wanted_smem, wanted_vmem, order_vmem, order_smem, last_vmem, last_smem,
    first_back, staged, first_total,
    send_sems, recv_sems, column_sems, row_sems, local_sem, input_sems,
):
    devices = groups * members
    others = devices - 1
    local_count = geo_blocks.shape[0]
    grp = lax.axis_index("grp")
    dev = lax.axis_index("dev")
    me = grp * members + dev
    member_bits = members.bit_length() - 1
    side_bits = side.bit_length() - 1

    def partner_of(step):
        shift = (step * 53) & (devices - 1)
        dg, dv = shift >> member_bits, shift & (members - 1)
        y = ((grp >> 1) + (dg >> 1)) & (groups // 2 - 1)
        core = (grp + dg) & 1
        x = ((dev >> side_bits) + (dv >> side_bits)) & (side - 1)
        z = (dev + dv) & (side - 1)
        return y * 2 + core, x * side + z

    my_y, my_core, my_x, my_z = grp >> 1, grp & 1, dev >> side_bits, dev & (side - 1)

    def at(dy, core, dx, dz):
        y = (my_y + dy) & (groups // 2 - 1)
        x, z = (my_x + dx) & (side - 1), (my_z + dz) & (side - 1)
        return y * 2 + ((my_core + core) & 1), x * side + z

    def in_column(which, index):
        return at(index >> 1, index & 1, which >> side_bits, which & (side - 1))

    my_key = dev * groups + grp
    my_rows = pl.ds(dev * groups, groups)

    def at_step(step, body):
        place = partner_of(step)
        body(step, place, place[0] * members + place[1])

    def two_steps(passes, body):
        @pl.loop(0, passes)
        def _(index):
            for step in (2 * index + 1, 2 * index + 2):
                at_step(step, body)

    def send(source, target, which, place):
        pltpu.make_async_remote_copy(
            src_ref=source, dst_ref=target,
            send_sem=send_sems.at[which], recv_sem=recv_sems.at[which],
            device_id=place, device_id_type=MESH,
        ).start()

    def drain(source, target, which):
        return pltpu.make_async_remote_copy(
            src_ref=source, dst_ref=target,
            send_sem=send_sems.at[which], recv_sem=recv_sems.at[which],
            device_id=(grp, dev), device_id_type=MESH,
        )

    barrier = pltpu.get_barrier_semaphore()
    for which in range(1, members):
        pl.semaphore_signal(barrier, inc=1, device_id=in_column(which, 0), device_id_type=MESH)
    for index in range(1, groups):
        pl.semaphore_signal(barrier, inc=1, device_id=in_column(0, index), device_id_type=MESH)

    inputs = [
        pltpu.make_async_copy(source, target, input_sems.at[index])
        for index, (source, target) in enumerate((
            (pair_hbm, pair_ref), (kind_hbm, kind_ref), (geo_hbm, geo_ref), (modes_hbm, modes_ref),
        ))
    ]
    for copy in inputs:
        copy.start()
    inputs[0].wait()
    inputs[1].wait()
    table, request = slot_table(pair_ref[...], kind_ref[...], local_count)
    row_vmem[...] = request
    asked_vmem[my_key] = request
    code_vmem[...] = table
    local = pltpu.make_async_copy(code_vmem, code_smem, local_sem)
    local.start()
    pl.semaphore_wait(barrier, members + groups - 2)

    for index in range(1, groups):
        send(row_vmem, asked_vmem.at[my_key], 0, in_column(0, index))
    in_own = drain(asked_vmem.at[pl.ds(0, groups - 1)], asked_vmem.at[pl.ds(0, groups - 1)], 0)
    high_rows = lax.broadcasted_iota(jnp.int32, (4, P_SIZE), 0)
    steps = jnp.where(high_rows < 3, X_STEPS, A_STEPS)
    inputs[2].wait()
    inputs[3].wait()
    for cluster in range(local_count):
        panels = slice(cluster * P_SIZE, (cluster + 1) * P_SIZE)
        mode_blocks[0, cluster] = modes_ref[0:HALF, panels]
        mode_blocks[1, cluster] = modes_ref[HALF : 2 * HALF, panels]
        geo_blocks[cluster] = jnp.round(geo_ref[:, panels] * steps)
    local.wait()
    in_own.wait_recv()

    def across(which, mark):
        return pltpu.make_async_remote_copy(
            src_ref=asked_vmem.at[my_rows], dst_ref=asked_vmem.at[my_rows],
            send_sem=send_sems.at[1], recv_sem=column_sems.at[mark],
            device_id=in_column(which, 0), device_id_type=MESH,
        )

    def readable(which):
        rows = pl.ds(in_column(which, 0)[1] * groups, groups)
        return pltpu.make_async_copy(asked_vmem.at[rows], asked_smem.at[rows], row_sems.at[which])

    for which in range(1, members):
        back_x, back_z = -(which // side) % side, -which % side
        across(which, back_x * side + back_z).start()
    local = readable(0)
    local.start()
    local.wait()

    def wanted(to, rank):
        key = (to & (members - 1)) * groups + (to >> member_bits)
        return (asked_smem[key, 0, me] >> (6 * rank)) & 63

    def geo_for(to):
        both = jnp.concatenate([geo_blocks[wanted(to, 0)], geo_blocks[wanted(to, 1)]], axis=0)
        both = jnp.concatenate([both[:, :128], both[:, 128:]], axis=0)
        return both.astype(jnp.int32).astype(jnp.int16)

    def send_geo(step, place, to):
        geo_stage[to] = geo_for(to)
        send(geo_stage.at[to], geo_got.at[me], 2, place)

    def send_modes(half, got):
        def body(step, place, to):
            for rank in range(2):
                mode_stage[half, 2 * to + rank] = mode_blocks[half, wanted(to, rank)]
            send(
                mode_stage.at[half, pl.ds(2 * to, 2)], got.at[pl.ds(2 * me, 2)], 3 + half, place
            )
        return body

    def at_place(place, body):
        body(0, place, place[0] * members + place[1])

    send_first = send_modes(0, first_got)
    send_second = send_modes(1, second_got)

    for body in (send_geo,):
        @pl.loop(1, groups)
        def _(index):
            at_place(in_column(0, index), body)

    def geos_for(which):
        readable(which).wait()

        @pl.loop(0, groups // 2)
        def _(index):
            at_place(in_column(which, 2 * index), send_geo)
            at_place(in_column(which, 2 * index + 1), send_geo)

    across(1, 1).wait_recv()
    readable(1).start()

    @pl.loop(1, members - 1)
    def _(which):
        across(which + 1, which + 1).wait_recv()
        readable(which + 1).start()
        geos_for(which)

    geos_for(members - 1)

    away = (members - 1) * groups
    for body in (send_first, send_second):
        @pl.loop(0, others // 2 + 1)
        def _(index):
            for step in (2 * index + 1, 2 * index + 2):
                @pl.when(step != devices)
                def _():
                    at_step(step, body)

    geo_got[me] = geo_for(me)
    for rank in range(2):
        first_got[2 * me + rank] = mode_blocks[0, wanted(me, rank)]
        second_got[2 * me + rank] = mode_blocks[1, wanted(me, rank)]

    @pl.loop(0, devices)
    def _(to):
        for rank in range(2):
            cluster = wanted(to, rank)
            wanted_smem[0, 2 * to + rank] = cluster

    def move(source, target):
        copy = pltpu.make_async_copy(source, target, local_sem)
        copy.start()
        copy.wait()

    geos = drain(geo_stage.at[pl.ds(0, others)], geo_got.at[pl.ds(0, others)], 2)
    geos.wait_recv()

    row = lax.broadcasted_iota(jnp.int32, (8, P_SIZE), 0)
    scale = jnp.where(
        (row & 3) < 3, FOUR_PI / X_STEPS, FOUR_PI * FOUR_PI / A_STEPS
    )

    def both_clusters(source):
        block = geo_got[source].astype(jnp.int32).astype(jnp.float32)
        return jnp.concatenate([block[0:8], block[8:16]], axis=1) * scale

    def length(block, factor):
        square = block * block
        return square[0:1] + square[1:2] + square[2:3] + block[3:4] * factor

    def tile_of(to, rank):
        code = code_smem[0, 2 * to + rank]
        other = (code >> 6) & 255
        factor = jnp.where((code & 16384) != 0, jnp.float32(0.1), jnp.float32(1.0))
        mine = both_clusters(to)
        theirs = both_clusters(other >> 1)
        if rank == 1:
            mine = pltpu.roll(mine, 4, 0)
        theirs = jnp.where((other & 1) == 1, pltpu.roll(theirs, 4, 0), theirs)
        norm = length(mine, factor)
        right = jnp.where(row < 3, mine, jnp.where(row == 3, norm, jnp.where(row == 4, 1.0, 0.0)))
        norm = length(theirs, factor)
        left = jnp.where(
            row < 3, -2.0 * theirs, jnp.where(row == 3, 1.0, jnp.where(row == 4, norm, 0.0))
        )
        a, b, c = thirds(left)
        left = jnp.concatenate([a, b, a, b, c, a], axis=0).astype(jnp.bfloat16)
        a, b, c = thirds(right)
        right = jnp.concatenate([a, a, b, b, a, c], axis=0).astype(jnp.bfloat16)
        squared = lax.dot_general(
            left, right, (((0,), (0,)), ((), ())), preferred_element_type=jnp.float32
        )
        return lax.rsqrt(squared).astype(jnp.bfloat16)

    def make_tiles(step, place, to):
        for rank in range(2):
            tiles[2 * (step - 1) + rank] = tile_of(to, rank)

    two_steps(devices // 2, make_tiles)

    def product(half, got, step, to, rank):
        code = code_smem[0, 2 * to + rank]
        keep = ((code >> 15) & 1).astype(jnp.float32)
        out = jnp.dot(
            got[(code >> 6) & 255], tiles[2 * (step - 1) + rank], preferred_element_type=jnp.float32
        )
        mode_back[half, 2 * to + rank] = (out * keep).astype(jnp.bfloat16)

    backs = (first_back, back_ref)

    def return_half(half, got):
        def give_back(to, place):
            send(
                mode_back.at[half, pl.ds(2 * to, 2)], backs[half].at[pl.ds(2 * me, 2)],
                5 + half, place,
            )

        def two_products(first, second):
            places = []
            for step in (first, second):
                place = partner_of(step)
                to = place[0] * members + place[1]
                places.append((to, place))
                for rank in range(2):
                    product(half, got, step, to, rank)
            return places

        @pl.loop(0, devices // 2 - 1)
        def _(index):
            for to, place in two_products(2 * index + 1, 2 * index + 2):
                give_back(to, place)

        give_back(*two_products(others, devices)[0])

    gots = []
    for half, got in enumerate((first_got, second_got)):
        arrived = drain(
            mode_stage.at[half, pl.ds(0, 2 * others)], got.at[pl.ds(0, 2 * others)], 3 + half
        )
        arrived.wait_recv()
        gots.append(arrived)
        return_half(half, got)

    for rank in range(2):
        first_back[2 * me + rank] = mode_back[0, 2 * me + rank]
    move(mode_back.at[1, pl.ds(2 * me, 2)], back_ref.at[pl.ds(2 * me, 2)])

    move(wanted_smem, wanted_vmem)
    move(wanted_vmem, wanted_ref)
    order_vmem[...], last_vmem[...] = sum_table(wanted_vmem[...], local_count)
    move(order_vmem, order_smem)
    move(last_vmem, last_smem)
    returned = [
        drain(mode_back.at[half, pl.ds(0, 2 * others)], backs[half].at[pl.ds(0, 2 * others)], 5 + half)
        for half in range(2)
    ]
    returned[0].wait_recv()

    def add(index, total):
        code = order_smem[0, index]
        total = total * (code >> 8).astype(jnp.float32) + first_back[code & 255].astype(jnp.float32)
        staged[index] = total
        return total

    lax.fori_loop(0, 2 * devices, add, jnp.zeros((HALF, P_SIZE), jnp.float32), unroll=4)
    for cluster in range(local_count):
        code = last_smem[0, cluster]
        first_total[:, cluster * P_SIZE : (cluster + 1) * P_SIZE] = (
            staged[code & 255] * (code >> 8).astype(jnp.float32)
        )
    move(first_total, total_ref)
    returned[1].wait_recv()
    for copy in returned:
        copy.wait_send()
    in_own.wait_send()
    others_rows = asked_vmem.at[pl.ds(0, away)]
    drain(others_rows, others_rows, 1).wait_send()
    geos.wait_send()
    for arrived in gots:
        arrived.wait_send()


def sum_kernel(
    chunks, wanted_hbm, back_ref, total_ref, out_ref, wanted_ref, arrived, first, second, in_sems, out_sems
):
    ends = back_ref.shape[0]
    count = ends // chunks

    def piece(chunk):
        part = pl.ds(chunk * count, count)
        return pltpu.make_async_copy(back_ref.at[part], arrived.at[part], in_sems.at[chunk])

    known = pltpu.make_async_copy(wanted_hbm, wanted_ref, in_sems.at[chunks + 1])
    known.start()
    for chunk in range(chunks):
        piece(chunk).start()
    ready = pltpu.make_async_copy(total_ref, first, in_sems.at[chunks])
    ready.start()
    written = [
        pltpu.make_async_copy(first, out_ref.at[pl.ds(0, HALF)], out_sems.at[0]),
        pltpu.make_async_copy(second, out_ref.at[pl.ds(HALF, HALF)], out_sems.at[1]),
    ]
    second[...] = jnp.zeros_like(second)
    known.wait()
    for chunk in range(chunks):
        piece(chunk).wait()

        @pl.loop(0, count, unroll=8)
        def _(index):
            slot = chunk * count + index
            place = pl.ds(pl.multiple_of(wanted_ref[0, slot] * P_SIZE, P_SIZE), P_SIZE)
            second[:, place] += arrived[slot].astype(jnp.float32)

        if chunk == 1:
            ready.wait()
            written[0].start()

    written[1].start()
    for copy in written:
        copy.wait()


def local(modes, geometry, pair_list, pair_kind):
    groups = lax.axis_size("grp")
    members = lax.axis_size("dev")
    devices = groups * members
    side = math.isqrt(members)
    local_count = modes.shape[1] // P_SIZE
    slots = pair_list.shape[0]
    ends = 2 * slots

    anywhere = pl.BlockSpec(memory_space=pl.ANY)
    back, total, wanted = pl.pallas_call(
        functools.partial(exchange_kernel, groups, members, side),
        out_shape=[
            jax.ShapeDtypeStruct((ends, HALF, P_SIZE), jnp.bfloat16),
            jax.ShapeDtypeStruct((HALF, local_count * P_SIZE), jnp.float32),
            jax.ShapeDtypeStruct((1, ends), jnp.int32),
        ],
        in_specs=[anywhere, anywhere, anywhere, anywhere],
        out_specs=[anywhere, anywhere, anywhere],
        scratch_shapes=[
            pltpu.VMEM((2, slots), jnp.int32),
            pltpu.VMEM((1, slots), jnp.int32),
            pltpu.VMEM(modes.shape, modes.dtype),
            pltpu.VMEM(geometry.shape, geometry.dtype),
            pltpu.VMEM((1, ends), jnp.int32),
            pltpu.SMEM((1, ends), jnp.int32),
            pltpu.VMEM((1, 128), jnp.int32),
            pltpu.VMEM((devices, 1, 128), jnp.int32),
            pltpu.SMEM((devices, 1, 128), jnp.int32),
            pltpu.VMEM((2, local_count, HALF, P_SIZE), jnp.bfloat16),
            pltpu.VMEM((local_count, 4, P_SIZE), jnp.float32),
            pltpu.VMEM((devices, 16, 128), jnp.int16),
            pltpu.VMEM((devices, 16, 128), jnp.int16),
            pltpu.VMEM((2, ends, HALF, P_SIZE), jnp.bfloat16),
            pltpu.VMEM((ends, HALF, P_SIZE), jnp.bfloat16),
            pltpu.VMEM((ends, HALF, P_SIZE), jnp.bfloat16),
            pltpu.VMEM((2, ends, HALF, P_SIZE), jnp.bfloat16),
            pltpu.VMEM((ends, P_SIZE, P_SIZE), jnp.bfloat16),
            pltpu.SMEM((1, ends), jnp.int32),
            pltpu.VMEM((1, ends), jnp.int32),
            pltpu.VMEM((1, ends), jnp.int32),
            pltpu.SMEM((1, ends), jnp.int32),
            pltpu.VMEM((1, 128), jnp.int32),
            pltpu.SMEM((1, 128), jnp.int32),
            pltpu.VMEM((ends, HALF, P_SIZE), jnp.bfloat16),
            pltpu.VMEM((ends, HALF, P_SIZE), jnp.float32),
            pltpu.VMEM((HALF, local_count * P_SIZE), jnp.float32),
            pltpu.SemaphoreType.DMA((7,)),
            pltpu.SemaphoreType.DMA((7,)),
            pltpu.SemaphoreType.DMA((members,)),
            pltpu.SemaphoreType.DMA((members,)),
            pltpu.SemaphoreType.DMA,
            pltpu.SemaphoreType.DMA((4,)),
        ],
        compiler_params=pltpu.CompilerParams(
            collective_id=0, has_side_effects=True, vmem_limit_bytes=58 * 1024 * 1024
        ),
    )(pair_list.T, pair_kind.reshape(1, slots), modes, geometry)

    chunks = 4
    return pl.pallas_call(
        functools.partial(sum_kernel, chunks),
        out_shape=jax.ShapeDtypeStruct((2 * HALF, local_count * P_SIZE), jnp.float32),
        in_specs=[anywhere, anywhere, anywhere],
        out_specs=anywhere,
        scratch_shapes=[
            pltpu.SMEM((1, ends), jnp.int32),
            pltpu.VMEM((ends, HALF, P_SIZE), jnp.bfloat16),
            pltpu.VMEM((HALF, local_count * P_SIZE), jnp.float32),
            pltpu.VMEM((HALF, local_count * P_SIZE), jnp.float32),
            pltpu.SemaphoreType.DMA((chunks + 2,)),
            pltpu.SemaphoreType.DMA((2,)),
        ],
        compiler_params=pltpu.CompilerParams(vmem_limit_bytes=58 * 1024 * 1024),
    )(wanted, back, total)


def solution(mesh):
    placed = (
        P(None, ("grp", "dev")),
        P(None, ("grp", "dev")),
        P(("grp", "dev"), None),
        P(("grp", "dev")),
    )
    return jax.shard_map(
        local, mesh=mesh, in_specs=placed, out_specs=P(None, ("grp", "dev")), check_vma=False
    )
```
